128 devices in a mesh: layer: 8 (over x_hi, y), query: 16 (over z, x_lo, core).
Axes of the slice: x: 4 (x_hi: 2, x_lo: 2; x = x_hi * 2 + x_lo), y: 4, z: 4, core: 2. Of those that a mesh axis runs over, the one named last changes fastest.
Arguments:
- train_grads: bfloat16 [256, 160, 4096], P('query', 'layer'), may hold values from -6 to 6
- query_pre: bfloat16 [1024, 160, 4096], P('query', 'layer'), may hold values from -0.0078125 to 0.0078125
- basis_in: bfloat16 [160, 64, 64], P('layer'), may hold values from -0.75 to 0.75
- basis_out: bfloat16 [160, 64, 64], P('layer'), may hold values from -0.75 to 0.75
Outputs:
- scores: float32 [256, 1024], P('layer', 'query')
The draws below stay inside these ranges and needn't reach their ends.
All inputs are finite; a program needn't handle non-finite values.
Results may differ from the reference program's by a relative error of at most 0.004.
Values may be sent and summed in bfloat16 or wider, within the bound.
A program may use at most 192 MiB of HBM per device.

```python
import jax
import jax.numpy as jnp
from jax import lax

K = 64
MODS = 160
TRAIN = 256
QUERIES = 1024


def level_of(own_key, shape, split, low, top_value):
    def one(position, parts):
        draws = jax.random.uniform(jax.random.fold_in(jax.random.fold_in(own_key, 6), position), (parts,), jnp.float32, low / len(split), top_value / len(split))
        return jnp.repeat(jnp.exp(draws), shape[position] // parts).reshape((-1,) + (1,) * (len(shape) - position - 1))

    gain = one(*split[0])
    for cut in split[1:]:
        gain = gain * one(*cut)
    return gain


def scatter_about(key, shape, spread, most, cuts=(), held_as=jnp.bfloat16):
    factor_of = level_of(key, shape, cuts, -0.22, 0.18) if cuts else 1.0
    entries = jax.random.normal(key, shape, jnp.float32) * spread * factor_of
    return jnp.minimum(jnp.maximum(entries, -most), most).astype(held_as)


def setup_inputs(seed: int = 0) -> dict:
    key_of = jax.random.split(jax.random.key(seed), 5)
    train_grads = scatter_about(key_of[0], (TRAIN, MODS, K * K), 1.0, 6.0, ((0, 16), (1, 8)))
    query_pre = scatter_about(key_of[1], (QUERIES, MODS, K * K), (MODS * K * K) ** -0.5, 0.0078125, ((0, 16), (1, 8)))
    basis_in = scatter_about(key_of[2], (MODS, K, K), K ** -0.5, 0.75, ((0, 8),))
    basis_out = scatter_about(key_of[3], (MODS, K, K), K ** -0.5, 0.75, ((0, 8),))
    return dict(train_grads=train_grads, query_pre=query_pre, basis_in=basis_in, basis_out=basis_out)


def reference(train_grads, query_pre, basis_in, basis_out):
    def module_step(totals, items):
        grads_block, query_block, inner_basis, outer_basis = items
        matrices = grads_block.reshape(TRAIN, K, K).astype(jnp.float32)
        half = jnp.einsum("eoi,ij->eoj", matrices, inner_basis.astype(jnp.float32)).astype(jnp.bfloat16)
        rotated = jnp.einsum("op,eoj->epj", outer_basis.astype(jnp.float32), half.astype(jnp.float32)).astype(jnp.bfloat16)
        partial_scores = jnp.dot(rotated.reshape(TRAIN, K * K), query_block.T, preferred_element_type=jnp.float32)
        return totals + partial_scores, None

    init = jnp.zeros((TRAIN, QUERIES), jnp.float32)
    totals, unused = lax.scan(module_step, init, (jnp.transpose(train_grads, (1, 0, 2)), jnp.transpose(query_pre, (1, 0, 2)), basis_in, basis_out))
    return totals
```

```python
import jax
import jax.numpy as jnp
from jax import lax
from jax.experimental import pallas as pl
from jax.experimental.pallas import tpu as pltpu
from jax.sharding import PartitionSpec as P

MESH = pl.DeviceIdType.MESH
BF16 = jnp.bfloat16
F32 = jnp.float32

WIDTH = 64
FLAT = WIDTH * WIDTH
MODULES = 20
OWN_TRAIN = 16
OWN_QUERY = 64
LAYERS = 8
DEPTH = 4
PAIR_SLOTS = 3
COLUMN_SLOTS = 4
SLOTS = PAIR_SLOTS + COLUMN_SLOTS
LANES = 128
CHUNKS = FLAT // LANES
PARTNERS = ((0, 1), (1, 0), (1, 1))


def dot(a, b):
    return jnp.dot(a, b, preferred_element_type=F32)


def dot_t(a, b):
    return lax.dot_general(a, b, (((1,), (1,)), ((), ())), preferred_element_type=F32)


def iota(shape, dim):
    return lax.broadcasted_iota(jnp.int32, shape, dim)


def one_hot(condition):
    return jnp.where(condition, 1.0, 0.0).astype(BF16)


def kernel(
    train_hbm, query_hbm, inner_ref, outer_ref, out_ref,
    train, query, padded, padded_query, swapped, rotated, queries, blocks, pair_queries, column_queries,
    swap, spread_rows, spread_lanes, keep, columns_of, rows_even, rows_odd,
    pair_scores, column_scores, mine, theirs, gathered, total, sib_total,
    train_sem, query_sem, local_sem, local_query_sem,
    block_send, block_recv, ring_send, ring_recv, half_send, half_recv,
    query_send, query_recv, pair_send, pair_recv, layer_send, layer_recv, core_send, core_recv,
):
    layer = lax.axis_index("layer")
    place = lax.axis_index("query")
    z = place // 4
    column = (place // 2) % 2
    core = place % 2
    here = place % 4

    def at_plane(other_column, other_core):
        x = 1 - column if other_column else column
        c = 1 - core if other_core else core
        return x, c, (layer, z * 4 + x * 2 + c)

    def at_ring(step):
        return (layer, ((z + step + DEPTH) % DEPTH) * 4 + here)

    load_train = pltpu.make_async_copy(train_hbm, train, train_sem)
    load_train.start()

    def load_query(part):
        return pltpu.make_async_copy(
            query_hbm.at[pl.ds(part * 16, 16)], query.at[part % 2], query_sem.at[part % 2]
        )

    load_query(0).start()
    load_query(1).start()

    barrier = pltpu.get_barrier_semaphore()
    for partner in PARTNERS:
        pl.semaphore_signal(barrier, inc=1, device_id=at_plane(*partner)[2], device_id_type=MESH)
    for step in (1, -1):
        pl.semaphore_signal(barrier, inc=1, device_id=at_ring(step), device_id_type=MESH)
    for step in range(1, LAYERS):
        pl.semaphore_signal(
            barrier, inc=1, device_id=((layer + step) % LAYERS, place), device_id_type=MESH
        )

    row, col = iota((256, 256), 0), iota((256, 256), 1)
    swap[...] = one_hot((row // 16 == col % 16) & (row % 16 == col // 16))
    row, col = iota((128, 64), 0), iota((128, 64), 1)
    spread_rows[...] = one_hot(row % 64 == col)
    row, col = iota((64, 256), 0), iota((64, 256), 1)
    spread_lanes[...] = one_hot(col % 64 == row)
    row, col = iota((128, 256), 0), iota((128, 256), 1)
    group = col // 64
    keep[...] = jnp.where(((group == 0) | (group == 3)) == (row < 64), 1.0, 0.0)
    row, col = iota((64, 64), 0), iota((64, 64), 1)
    columns_of[...] = one_hot(col == 2 * (row % 32) + row // 32)
    rows_even[...] = one_hot(row == 2 * (col % 32) + col // 32)
    rows_odd[...] = one_hot(row == 2 * (col % 32) + 1 - col // 32)
    padded[...] = jnp.zeros_like(padded)
    padded_query[...] = jnp.zeros_like(padded_query)

    pl.semaphore_wait(barrier, len(PARTNERS) + 2 + LAYERS - 1)

    def store_swapped(first, count, example, value):
        pieces = jnp.concatenate(
            [
                jnp.concatenate(
                    [value[:, (16 * half + c) * LANES:(16 * half + c + 1) * LANES] for c in range(16)], axis=0
                )
                for half in range(2)
            ],
            axis=1,
        )
        turned = dot(swap[0:16 * count, :], pieces).astype(BF16)
        for m in range(count):
            for half in range(2):
                swapped[first + m, example, 16 * half:16 * half + 16, :] = turned[
                    16 * m:16 * m + 16, half * LANES:(half + 1) * LANES
                ]

    def turn_train(example, carry):
        store_swapped(0, 16, example, train[example, 0:16, :])
        return carry

    def turn_train_rest(example, carry):
        padded[0:4, :] = train[example, 16:20, :]
        store_swapped(16, 4, example, padded[...])
        return carry

    def rotate(m, carry):
        inner = dot(dot(spread_rows[...], inner_ref[m]).astype(BF16), spread_lanes[...])
        inner = (inner * keep[...]).astype(BF16)
        turned = dot_t(columns_of[...], outer_ref[m]).astype(BF16)
        outer = jnp.where(
            iota((64, 64), 0) < 32, dot(turned, rows_even[...]), dot(turned, rows_odd[...])
        ).astype(BF16)
        half = dot(swapped[m].reshape(512, LANES), inner).astype(BF16)
        stacked = jnp.concatenate(
            [
                jnp.concatenate(
                    [half[32 * e:32 * e + 32, h * LANES:(h + 1) * LANES] for e in range(OWN_TRAIN)], axis=1
                )
                for h in range(2)
            ],
            axis=0,
        )
        both = dot(outer, stacked)
        first = iota((32, OWN_TRAIN * LANES), 1) % LANES < WIDTH
        result = jnp.where(first, both[:32], both[32:]).astype(BF16)
        pieces = jnp.concatenate(
            [
                jnp.concatenate(
                    [result[16 * h:16 * h + 16, e * LANES:(e + 1) * LANES] for e in range(OWN_TRAIN)], axis=0
                )
                for h in range(2)
            ],
            axis=1,
        )
        final = dot(swap[...], pieces).astype(BF16)
        rotated[m] = jnp.concatenate(
            [final[16 * c:16 * c + 16, h * LANES:(h + 1) * LANES] for h in range(2) for c in range(16)], axis=1
        )
        return carry

    def turn_query(part):
        load_query(part).wait()
        slot = part % 2
        rows = pl.ds(pl.multiple_of(part * 16, 16), 16)

        def lanes_step(step, carry):
            lanes = pl.ds(pl.multiple_of(step * 256, 256), 256)
            turned = dot(swap[...], query[slot, :, 0:16, lanes].reshape(256, 256)).astype(BF16)
            for m in range(16):
                queries[m, rows, lanes] = turned[16 * m:16 * m + 16]
            for q in range(16):
                padded_query[q, 0:4, :] = query[slot, q, 16:20, lanes]
            turned = dot(swap[0:64, :], padded_query[...].reshape(256, 256)).astype(BF16)
            for m in range(4):
                queries[16 + m, rows, lanes] = turned[16 * m:16 * m + 16]
            return carry

        lax.fori_loop(0, FLAT // 256, lanes_step, 0)

    def block_copy(slot, partner):
        x, c, device = at_plane(*PARTNERS[partner])
        m = 4 * slot + 2 * x + c if slot < PAIR_SLOTS else 6 + 2 * slot + c
        return pltpu.make_async_remote_copy(
            src_ref=rotated.at[m],
            dst_ref=blocks.at[slot, z, pl.ds(pl.multiple_of(here * 16, 16), 16)],
            send_sem=block_send.at[slot, partner],
            recv_sem=block_recv.at[slot, partner],
            device_id=device,
            device_id_type=MESH,
        )

    def own_copy(slot):
        m = 4 * slot + here if slot < PAIR_SLOTS else 6 + 2 * slot + core
        return pltpu.make_async_copy(
            rotated.at[m], blocks.at[slot, z, pl.ds(pl.multiple_of(here * 16, 16), 16)], local_sem.at[slot]
        )

    def ring_copy(slot, way):
        return pltpu.make_async_remote_copy(
            src_ref=blocks.at[slot, z],
            dst_ref=blocks.at[slot, z],
            send_sem=ring_send.at[slot, way],
            recv_sem=ring_recv.at[slot, way],
            device_id=at_ring(1 - 2 * way),
            device_id_type=MESH,
        )

    def half_copy(slot, way):
        source = (z + DEPTH - 1 + 2 * way) % DEPTH
        half = blocks.at[slot, source, pl.ds(32 * way, 32)]
        return pltpu.make_async_remote_copy(
            src_ref=half,
            dst_ref=half,
            send_sem=half_send.at[slot, way],
            recv_sem=half_recv.at[slot, way],
            device_id=at_ring(1 - 2 * way),
            device_id_type=MESH,
        )

    def query_copy(slot, partner, part=None):
        x, c, device = at_plane(*PARTNERS[partner])
        rows = pl.ds(0, 64) if part is None else pl.ds(16 * part, 16)
        to = pl.ds(pl.multiple_of(core * 64, 64) if part is None else pl.multiple_of(core * 64 + part * 16, 16), 64 if part is None else 16)
        if slot < PAIR_SLOTS:
            m, target = 4 * slot + 2 * x + c, pair_queries.at[slot, PARTNERS[partner][0], to]
        else:
            m, target = 6 + 2 * slot + c, column_queries.at[slot - PAIR_SLOTS, to]
        return pltpu.make_async_remote_copy(
            src_ref=queries.at[m, rows],
            dst_ref=target,
            send_sem=query_send.at[slot, partner],
            recv_sem=query_recv.at[slot, partner],
            device_id=device,
            device_id_type=MESH,
        )

    def own_query_copy(slot):
        to = pl.ds(pl.multiple_of(core * 64, 64), 64)
        if slot < PAIR_SLOTS:
            m, target = 4 * slot + here, pair_queries.at[slot, 0, to]
        else:
            m, target = 6 + 2 * slot + core, column_queries.at[slot - PAIR_SLOTS, to]
        return pltpu.make_async_copy(queries.at[m], target, local_query_sem.at[slot])

    def send_blocks(slot):
        for partner in (1, 2, 0):
            block_copy(slot, partner).start()
        own_copy(slot).start()

    def send_ring(slot):
        for partner in range(3):
            block_copy(slot, partner).wait_recv()
        own_copy(slot).wait()
        for way in range(2):
            ring_copy(slot, way).start()

    def send_half(slot):
        for way in range(2):
            ring_copy(slot, way).wait_recv()
            half_copy(slot, way).start()

    def query_partners(slot):
        return (1, 2, 0) if slot < PAIR_SLOTS else (0,)

    def send_queries(part):
        for slot in range(PAIR_SLOTS):
            for partner in query_partners(slot):
                query_copy(slot, partner, part).start()

    load_train.wait()
    lax.fori_loop(0, OWN_TRAIN, turn_train, 0)
    lax.fori_loop(0, 4, rotate, 0)
    send_blocks(0)
    lax.fori_loop(4, 8, rotate, 0)
    send_blocks(1)
    send_ring(0)
    turn_query(0)
    load_query(2).start()
    send_queries(0)
    lax.fori_loop(8, 12, rotate, 0)
    send_blocks(2)
    send_ring(1)
    turn_query(1)
    load_query(3).start()
    send_queries(1)
    lax.fori_loop(0, OWN_TRAIN, turn_train_rest, 0)
    lax.fori_loop(12, 16, rotate, 0)
    send_blocks(3)
    send_blocks(4)
    send_ring(2)
    turn_query(2)
    send_queries(2)
    send_ring(3)
    lax.fori_loop(16, 20, rotate, 0)
    send_blocks(5)
    send_blocks(6)
    send_ring(4)
    turn_query(3)
    send_queries(3)
    for slot in range(PAIR_SLOTS, SLOTS):
        query_copy(slot, 0).start()
    for slot in range(SLOTS):
        own_query_copy(slot).start()
    send_ring(5)
    send_ring(6)
    for slot in range(SLOTS):
        send_half(slot)

    def wait_blocks(slot):
        for way in range(2):
            half_copy(slot, way).wait_recv()
        for partner in query_partners(slot):
            query_copy(slot, partner).wait_recv()
        own_query_copy(slot).wait()

    pair_scores[...] = jnp.zeros_like(pair_scores)
    column_scores[...] = jnp.zeros_like(column_scores)
    for slot in range(PAIR_SLOTS):
        wait_blocks(slot)

        def pair_step(step, carry):
            lanes = pl.ds(pl.multiple_of(step * 512, 512), 512)
            rows = blocks[slot, :, :, lanes].reshape(256, 512)
            for side in range(2):
                pair_scores[side] += dot_t(rows, pair_queries[slot, side, :, lanes])
            return carry

        lax.fori_loop(0, FLAT // 512, pair_step, 0)

    cross = pltpu.make_async_remote_copy(
        src_ref=pair_scores.at[1],
        dst_ref=theirs,
        send_sem=pair_send,
        recv_sem=pair_recv,
        device_id=at_plane(1, 0)[2],
        device_id_type=MESH,
    )
    cross.start()
    for slot in range(PAIR_SLOTS, SLOTS):
        wait_blocks(slot)

        def column_step(step, carry):
            lanes = pl.ds(pl.multiple_of(step * 512, 512), 512)
            rows = blocks[slot, :, :, lanes].reshape(256, 512)
            column_scores[...] += dot_t(rows, column_queries[slot - PAIR_SLOTS, :, lanes])
            return carry

        lax.fori_loop(0, FLAT // 512, column_step, 0)
    cross.wait_recv()
    mine[...] = (pair_scores[0] + column_scores[...] + theirs[...]).reshape(LAYERS, 32, LANES)

    def layer_copy(step):
        return pltpu.make_async_remote_copy(
            src_ref=mine.at[(layer + step) % LAYERS],
            dst_ref=gathered.at[step],
            send_sem=layer_send.at[step],
            recv_sem=layer_recv.at[step],
            device_id=((layer + step) % LAYERS, place),
            device_id_type=MESH,
        )

    for step in range(1, LAYERS):
        layer_copy(step).start()
    total[...] = mine[layer]
    for step in range(1, LAYERS):
        layer_copy(step).wait_recv()
        total[...] += gathered[step]
    between = pltpu.make_async_remote_copy(
        src_ref=total,
        dst_ref=sib_total,
        send_sem=core_send,
        recv_sem=core_recv,
        device_id=at_plane(0, 1)[2],
        device_id_type=MESH,
    )
    between.start()
    between.wait()
    both = total[...] + sib_total[...]
    out_ref[...] = jnp.where(core == 0, both[:, :WIDTH], both[:, WIDTH:])

    for step in range(1, LAYERS):
        layer_copy(step).wait_send()
    cross.wait_send()
    for slot in range(SLOTS):
        for partner in range(3):
            block_copy(slot, partner).wait_send()
        for partner in query_partners(slot):
            query_copy(slot, partner).wait_send()
        for way in range(2):
            ring_copy(slot, way).wait_send()
            half_copy(slot, way).wait_send()


def shards(train_grads, query_pre, basis_in, basis_out):
    dma = pltpu.SemaphoreType.DMA
    return pl.pallas_call(
        kernel,
        out_shape=jax.ShapeDtypeStruct((32, WIDTH), F32),
        in_specs=[
            pl.BlockSpec(memory_space=pl.ANY),
            pl.BlockSpec(memory_space=pl.ANY),
            pl.BlockSpec(memory_space=pltpu.VMEM),
            pl.BlockSpec(memory_space=pltpu.VMEM),
        ],
        out_specs=pl.BlockSpec(memory_space=pltpu.VMEM),
        scratch_shapes=[
            pltpu.VMEM((OWN_TRAIN, MODULES, FLAT), BF16),
            pltpu.VMEM((2, 16, MODULES, FLAT), BF16),
            pltpu.VMEM((16, FLAT), BF16),
            pltpu.VMEM((16, 16, 256), BF16),
            pltpu.VMEM((MODULES, OWN_TRAIN, CHUNKS, LANES), BF16),
            pltpu.VMEM((MODULES, OWN_TRAIN, FLAT), BF16),
            pltpu.VMEM((MODULES, OWN_QUERY, FLAT), BF16),
            pltpu.VMEM((SLOTS, DEPTH, 64, FLAT), BF16),
            pltpu.VMEM((PAIR_SLOTS, 2, 128, FLAT), BF16),
            pltpu.VMEM((COLUMN_SLOTS, 128, FLAT), BF16),
            pltpu.VMEM((256, 256), BF16),
            pltpu.VMEM((128, 64), BF16),
            pltpu.VMEM((64, 256), BF16),
            pltpu.VMEM((128, 256), F32),
            pltpu.VMEM((64, 64), BF16),
            pltpu.VMEM((64, 64), BF16),
            pltpu.VMEM((64, 64), BF16),
            pltpu.VMEM((2, 256, LANES), F32),
            pltpu.VMEM((256, LANES), F32),
            pltpu.VMEM((LAYERS, 32, LANES), F32),
            pltpu.VMEM((256, LANES), F32),
            pltpu.VMEM((LAYERS, 32, LANES), F32),
            pltpu.VMEM((32, LANES), F32),
            pltpu.VMEM((32, LANES), F32),
            dma, dma((2,)), dma((SLOTS,)), dma((SLOTS,)),
            dma((SLOTS, 3)), dma((SLOTS, 3)), dma((SLOTS, 2)), dma((SLOTS, 2)), dma((SLOTS, 2)), dma((SLOTS, 2)),
            dma((SLOTS, 3)), dma((SLOTS, 3)), dma, dma, dma((LAYERS,)), dma((LAYERS,)), dma, dma,
        ],
        compiler_params=pltpu.CompilerParams(
            collective_id=0, has_side_effects=True, vmem_limit_bytes=62 * 2**20
        ),
        name="influence_scores",
    )(train_grads, query_pre, basis_in, basis_out)


def solution(mesh):
    placed = (
        P("query", "layer", None),
        P("query", "layer", None),
        P("layer", None, None),
        P("layer", None, None),
    )
    return jax.shard_map(
        shards, mesh=mesh, in_specs=placed, out_specs=P("layer", "query"), check_vma=False
    )
```

```python
import jax
import jax.numpy as jnp
from jax import lax
from jax.experimental import pallas as pl
from jax.experimental.pallas import tpu as pltpu
from jax.sharding import PartitionSpec as P

MESH = pl.DeviceIdType.MESH
BF16 = jnp.bfloat16
F32 = jnp.float32

WIDTH = 64
FLAT = WIDTH * WIDTH
MODULES = 20
OWN_TRAIN = 16
LAYERS = 8
DEPTH = 4
PAIR_SLOTS = 3
COLUMN_SLOTS = 4
SLOTS = PAIR_SLOTS + COLUMN_SLOTS
LANES = 128
PARTNERS = ((0, 1), (1, 0), (1, 1))


def dot(a, b):
    return jnp.dot(a, b, preferred_element_type=F32)


def dot_t(a, b):
    return lax.dot_general(a, b, (((1,), (1,)), ((), ())), preferred_element_type=F32)


def iota(shape, dim):
    return lax.broadcasted_iota(jnp.int32, shape, dim)


def one_hot(condition):
    return jnp.where(condition, 1.0, 0.0).astype(BF16)


def kernel(
    train_hbm, query_hbm, inner_ref, outer_ref, out_ref,
    train, rotated, blocks, pair_queries, column_queries,
    swap, spread_rows, spread_lanes, keep, columns_of, rows_even, rows_odd,
    pair_scores, column_scores, mine, theirs, gathered, total, sib_total,
    train_sem, local_sem, local_query_sem,
    block_send, block_recv, ring_send, ring_recv, half_send, half_recv,
    query_send, query_recv, pair_send, pair_recv, layer_send, layer_recv, core_send, core_recv,
):
    layer = lax.axis_index("layer")
    place = lax.axis_index("query")
    z = place // 4
    column = (place // 2) % 2
    core = place % 2
    here = place % 4

    def at_plane(other_column, other_core):
        x = 1 - column if other_column else column
        c = 1 - core if other_core else core
        return x, c, (layer, z * 4 + x * 2 + c)

    def at_ring(step):
        return (layer, ((z + step + DEPTH) % DEPTH) * 4 + here)

    def load_train(m):
        return pltpu.make_async_copy(train_hbm.at[m], train.at[m], train_sem.at[m])

    def each_module(first, last, step):
        def body(m, carry):
            step(m)
            return carry

        lax.fori_loop(first, last, body, 0)

    each_module(0, MODULES, lambda m: load_train(m).start())

    barrier = pltpu.get_barrier_semaphore()
    for partner in PARTNERS:
        pl.semaphore_signal(barrier, inc=1, device_id=at_plane(*partner)[2], device_id_type=MESH)
    for step in (1, -1):
        pl.semaphore_signal(barrier, inc=1, device_id=at_ring(step), device_id_type=MESH)
    for step in range(1, LAYERS):
        pl.semaphore_signal(
            barrier, inc=1, device_id=((layer + step) % LAYERS, place), device_id_type=MESH
        )

    row, col = iota((256, 256), 0), iota((256, 256), 1)
    swap[...] = one_hot((row // 16 == col % 16) & (row % 16 == col // 16))
    row, col = iota((128, 64), 0), iota((128, 64), 1)
    spread_rows[...] = one_hot(row % 64 == col)
    row, col = iota((64, 256), 0), iota((64, 256), 1)
    spread_lanes[...] = one_hot(col % 64 == row)
    row, col = iota((128, 256), 0), iota((128, 256), 1)
    group = col // 64
    keep[...] = jnp.where(((group == 0) | (group == 3)) == (row < 64), 1.0, 0.0)
    row, col = iota((64, 64), 0), iota((64, 64), 1)
    columns_of[...] = one_hot(col == 2 * (row % 32) + row // 32)
    rows_even[...] = one_hot(row == 2 * (col % 32) + col // 32)
    rows_odd[...] = one_hot(row == 2 * (col % 32) + 1 - col // 32)

    pl.semaphore_wait(barrier, len(PARTNERS) + 2 + LAYERS - 1)

    def side_by_side(pieces):
        return jnp.concatenate(pieces, axis=1)

    def stack(pieces):
        return jnp.concatenate(pieces, axis=0)

    def swap_rows(tile):
        pieces = side_by_side([stack([tile(16 * half + c) for c in range(16)]) for half in range(2)])
        return dot(swap[...], pieces).astype(BF16)

    def rotate(m):
        inner = dot(dot(spread_rows[...], inner_ref[m]).astype(BF16), spread_lanes[...])
        inner = (inner * keep[...]).astype(BF16)
        turned = dot_t(columns_of[...], outer_ref[m]).astype(BF16)
        outer = jnp.where(
            iota((64, 64), 0) < 32, dot(turned, rows_even[...]), dot(turned, rows_odd[...])
        ).astype(BF16)
        load_train(m).wait()
        grads = train[m]
        rows = swap_rows(lambda c: grads[:, c * LANES:(c + 1) * LANES])
        matrices = stack(
            [rows[16 * e:16 * e + 16, h * LANES:(h + 1) * LANES] for e in range(OWN_TRAIN) for h in range(2)]
        )
        half = dot(matrices, inner).astype(BF16)
        stacked = stack(
            [
                side_by_side([half[32 * e:32 * e + 32, h * LANES:(h + 1) * LANES] for e in range(OWN_TRAIN)])
                for h in range(2)
            ]
        )
        both = dot(outer, stacked)
        first = iota((32, OWN_TRAIN * LANES), 1) % LANES < WIDTH
        result = jnp.where(first, both[:32], both[32:]).astype(BF16)
        pieces = side_by_side(
            [
                stack([result[16 * h:16 * h + 16, e * LANES:(e + 1) * LANES] for e in range(OWN_TRAIN)])
                for h in range(2)
            ]
        )
        final = dot(swap[...], pieces).astype(BF16)
        rotated[m] = side_by_side(
            [final[16 * c:16 * c + 16, h * LANES:(h + 1) * LANES] for h in range(2) for c in range(16)]
        )

    def block_copy(slot, partner):
        x, c, device = at_plane(*PARTNERS[partner])
        m = 4 * slot + 2 * x + c if slot < PAIR_SLOTS else 6 + 2 * slot + c
        return pltpu.make_async_remote_copy(
            src_ref=rotated.at[m],
            dst_ref=blocks.at[slot, z, pl.ds(pl.multiple_of(here * 16, 16), 16)],
            send_sem=block_send.at[slot, partner],
            recv_sem=block_recv.at[slot, partner],
            device_id=device,
            device_id_type=MESH,
        )

    def own_copy(slot):
        m = 4 * slot + here if slot < PAIR_SLOTS else 6 + 2 * slot + core
        return pltpu.make_async_copy(
            rotated.at[m], blocks.at[slot, z, pl.ds(pl.multiple_of(here * 16, 16), 16)], local_sem.at[slot]
        )

    def ring_copy(slot, way):
        return pltpu.make_async_remote_copy(
            src_ref=blocks.at[slot, z],
            dst_ref=blocks.at[slot, z],
            send_sem=ring_send.at[slot, way],
            recv_sem=ring_recv.at[slot, way],
            device_id=at_ring(1 - 2 * way),
            device_id_type=MESH,
        )

    def half_copy(slot, way):
        source = (z + DEPTH - 1 + 2 * way) % DEPTH
        half = blocks.at[slot, source, pl.ds(32 * way, 32)]
        return pltpu.make_async_remote_copy(
            src_ref=half,
            dst_ref=half,
            send_sem=half_send.at[slot, way],
            recv_sem=half_recv.at[slot, way],
            device_id=at_ring(1 - 2 * way),
            device_id_type=MESH,
        )

    def query_copy(slot, partner):
        x, c, device = at_plane(*PARTNERS[partner])
        to = pl.ds(pl.multiple_of(core * 64, 64), 64)
        if slot < PAIR_SLOTS:
            m, target = 4 * slot + 2 * x + c, pair_queries.at[slot, PARTNERS[partner][0], to]
        else:
            m, target = 6 + 2 * slot + c, column_queries.at[slot - PAIR_SLOTS, to]
        return pltpu.make_async_remote_copy(
            src_ref=query_hbm.at[m],
            dst_ref=target,
            send_sem=query_send.at[slot, partner],
            recv_sem=query_recv.at[slot, partner],
            device_id=device,
            device_id_type=MESH,
        )

    def own_query_copy(slot):
        to = pl.ds(pl.multiple_of(core * 64, 64), 64)
        if slot < PAIR_SLOTS:
            m, target = 4 * slot + here, pair_queries.at[slot, 0, to]
        else:
            m, target = 6 + 2 * slot + core, column_queries.at[slot - PAIR_SLOTS, to]
        return pltpu.make_async_copy(query_hbm.at[m], target, local_query_sem.at[slot])

    def send_blocks(slot):
        for partner in (1, 2, 0):
            block_copy(slot, partner).start()
        own_copy(slot).start()

    def send_ring(slot):
        for partner in range(3):
            block_copy(slot, partner).wait_recv()
        own_copy(slot).wait()
        for way in range(2):
            ring_copy(slot, way).start()

    def send_half(slot):
        for way in range(2):
            ring_copy(slot, way).wait_recv()
            half_copy(slot, way).start()

    def query_partners(slot):
        return (1, 2, 0) if slot < PAIR_SLOTS else (0,)

    def send_queries(slot):
        for partner in query_partners(slot):
            query_copy(slot, partner).start()
        own_query_copy(slot).start()

    for slot in range(SLOTS):
        if slot < PAIR_SLOTS:
            each_module(4 * slot, 4 * slot + 4, rotate)
        else:
            each_module(6 + 2 * slot, 8 + 2 * slot, rotate)
        send_blocks(slot)
        if slot > 0:
            send_ring(slot - 1)
    for slot in range(SLOTS):
        send_queries(slot)
    send_ring(SLOTS - 1)
    for slot in range(SLOTS):
        send_half(slot)

    def wait_blocks(slot):
        for way in range(2):
            half_copy(slot, way).wait_recv()
        for partner in query_partners(slot):
            query_copy(slot, partner).wait_recv()
        own_query_copy(slot).wait()

    pair_scores[...] = jnp.zeros_like(pair_scores)
    column_scores[...] = jnp.zeros_like(column_scores)

    def score_pair(slot):
        wait_blocks(slot)

        def pair_step(step, carry):
            lanes = pl.ds(pl.multiple_of(step * 512, 512), 512)
            rows = blocks[slot, :, :, lanes].reshape(256, 512)
            for side in range(2):
                pair_scores[side] += dot_t(rows, pair_queries[slot, side, :, lanes])
            return carry

        lax.fori_loop(0, FLAT // 512, pair_step, 0)

    def score_column(slot):
        wait_blocks(slot)

        def column_step(step, carry):
            lanes = pl.ds(pl.multiple_of(step * 512, 512), 512)
            rows = blocks[slot, :, :, lanes].reshape(256, 512)
            column_scores[...] += dot_t(rows, column_queries[slot - PAIR_SLOTS, :, lanes])
            return carry

        lax.fori_loop(0, FLAT // 512, column_step, 0)

    score_pair(0)
    score_pair(1)
    score_column(3)
    score_column(4)
    score_pair(2)
    cross = pltpu.make_async_remote_copy(
        src_ref=pair_scores.at[1],
        dst_ref=theirs,
        send_sem=pair_send,
        recv_sem=pair_recv,
        device_id=at_plane(1, 0)[2],
        device_id_type=MESH,
    )
    cross.start()
    score_column(5)
    score_column(6)
    cross.wait_recv()
    mine[...] = (pair_scores[0] + column_scores[...] + theirs[...]).reshape(LAYERS, 32, LANES)

    def layer_copy(step):
        return pltpu.make_async_remote_copy(
            src_ref=mine.at[(layer + step) % LAYERS],
            dst_ref=gathered.at[step],
            send_sem=layer_send.at[step],
            recv_sem=layer_recv.at[step],
            device_id=((layer + step) % LAYERS, place),
            device_id_type=MESH,
        )

    for step in range(1, LAYERS):
        layer_copy(step).start()
    total[...] = mine[layer]
    for step in range(1, LAYERS):
        layer_copy(step).wait_recv()
        total[...] += gathered[step]
    between = pltpu.make_async_remote_copy(
        src_ref=total,
        dst_ref=sib_total,
        send_sem=core_send,
        recv_sem=core_recv,
        device_id=at_plane(0, 1)[2],
        device_id_type=MESH,
    )
    between.start()
    between.wait()
    both = total[...] + sib_total[...]
    out_ref[...] = jnp.where(core == 0, both[:, :WIDTH], both[:, WIDTH:])

    for step in range(1, LAYERS):
        layer_copy(step).wait_send()
    cross.wait_send()
    for slot in range(SLOTS):
        for partner in range(3):
            block_copy(slot, partner).wait_send()
        for partner in query_partners(slot):
            query_copy(slot, partner).wait_send()
        for way in range(2):
            ring_copy(slot, way).wait_send()
            half_copy(slot, way).wait_send()


def shards(train_grads, query_pre, basis_in, basis_out):
    dma = pltpu.SemaphoreType.DMA
    return pl.pallas_call(
        kernel,
        out_shape=jax.ShapeDtypeStruct((32, WIDTH), F32),
        in_specs=[
            pl.BlockSpec(memory_space=pl.ANY),
            pl.BlockSpec(memory_space=pl.ANY),
            pl.BlockSpec(memory_space=pltpu.VMEM),
            pl.BlockSpec(memory_space=pltpu.VMEM),
        ],
        out_specs=pl.BlockSpec(memory_space=pltpu.VMEM),
        scratch_shapes=[
            pltpu.VMEM((MODULES, OWN_TRAIN, FLAT), BF16),
            pltpu.VMEM((MODULES, OWN_TRAIN, FLAT), BF16),
            pltpu.VMEM((SLOTS, DEPTH, 64, FLAT), BF16),
            pltpu.VMEM((PAIR_SLOTS, 2, 128, FLAT), BF16),
            pltpu.VMEM((COLUMN_SLOTS, 128, FLAT), BF16),
            pltpu.VMEM((256, 256), BF16),
            pltpu.VMEM((128, 64), BF16),
            pltpu.VMEM((64, 256), BF16),
            pltpu.VMEM((128, 256), F32),
            pltpu.VMEM((64, 64), BF16),
            pltpu.VMEM((64, 64), BF16),
            pltpu.VMEM((64, 64), BF16),
            pltpu.VMEM((2, 256, LANES), F32),
            pltpu.VMEM((256, LANES), F32),
            pltpu.VMEM((LAYERS, 32, LANES), F32),
            pltpu.VMEM((256, LANES), F32),
            pltpu.VMEM((LAYERS, 32, LANES), F32),
            pltpu.VMEM((32, LANES), F32),
            pltpu.VMEM((32, LANES), F32),
            dma((MODULES,)), dma((SLOTS,)), dma((SLOTS,)),
            dma((SLOTS, 3)), dma((SLOTS, 3)), dma((SLOTS, 2)), dma((SLOTS, 2)), dma((SLOTS, 2)), dma((SLOTS, 2)),
            dma((SLOTS, 3)), dma((SLOTS, 3)), dma, dma, dma((LAYERS,)), dma((LAYERS,)), dma, dma,
        ],
        compiler_params=pltpu.CompilerParams(
            collective_id=0, has_side_effects=True, vmem_limit_bytes=62 * 2**20
        ),
        name="influence_scores",
    )(jnp.transpose(train_grads, (1, 0, 2)), jnp.transpose(query_pre, (1, 0, 2)), basis_in, basis_out)


def solution(mesh):
    placed = (
        P("query", "layer", None),
        P("query", "layer", None),
        P("layer", None, None),
        P("layer", None, None),
    )
    return jax.shard_map(
        shards, mesh=mesh, in_specs=placed, out_specs=P("layer", "query"), check_vma=False
    )
```

```python
import jax
import jax.numpy as jnp
from jax import lax
from jax.experimental import pallas as pl
from jax.experimental.pallas import tpu as pltpu
from jax.sharding import PartitionSpec as P

MESH = pl.DeviceIdType.MESH
BF16 = jnp.bfloat16
F32 = jnp.float32

WIDTH = 64
FLAT = WIDTH * WIDTH
MODULES = 20
OWN_TRAIN = 16
LAYERS = 8
DEPTH = 4
PAIR_SLOTS = 3
COLUMN_SLOTS = 4
SLOTS = PAIR_SLOTS + COLUMN_SLOTS
FIRST = PAIR_SLOTS
LAST = SLOTS - 1
LANES = 128
PARTNERS = ((0, 1), (1, 0), (1, 1))


def dot(a, b):
    return jnp.dot(a, b, preferred_element_type=F32)


def dot_t(a, b):
    return lax.dot_general(a, b, (((1,), (1,)), ((), ())), preferred_element_type=F32)


def iota(shape, dim):
    return lax.broadcasted_iota(jnp.int32, shape, dim)


def one_hot(condition):
    return jnp.where(condition, 1.0, 0.0).astype(BF16)


def kernel(
    train_hbm, query_hbm, inner_hbm, outer_hbm, out_ref,
    inner_ref, outer_ref,
    train, rotated, blocks, pair_queries, column_queries,
    swap, spread_rows, spread_lanes, keep, columns_of, rows_even, rows_odd,
    pair_scores, column_scores, theirs, packed, gathered,
    basis_sem, train_sem, local_sem, local_query_sem,
    block_send, block_recv, piece_send, piece_recv, ring_send, ring_recv, half_send, half_recv,
    query_send, query_recv, pair_send, pair_recv, layer_send, layer_recv,
):
    layer = lax.axis_index("layer")
    place = lax.axis_index("query")
    z = place // 4
    column = (place // 2) % 2
    core = place % 2
    here = place % 4

    def at_plane(other_column, other_core):
        x = 1 - column if other_column else column
        c = 1 - core if other_core else core
        return x, c, (layer, z * 4 + x * 2 + c)

    def at_ring(step):
        return (layer, ((z + step + DEPTH) % DEPTH) * 4 + here)

    def at_layer(step, other_core):
        c = 1 - core if other_core else core
        return ((layer + step) % LAYERS, z * 4 + column * 2 + c)

    barrier = pltpu.get_barrier_semaphore()
    for partner in PARTNERS:
        pl.semaphore_signal(barrier, inc=1, device_id=at_plane(*partner)[2], device_id_type=MESH)
    for step in (1, -1):
        pl.semaphore_signal(barrier, inc=1, device_id=at_ring(step), device_id_type=MESH)
    for step in range(1, LAYERS):
        for other in range(2):
            pl.semaphore_signal(barrier, inc=1, device_id=at_layer(step, other), device_id_type=MESH)

    def load_train(m):
        return pltpu.make_async_copy(train_hbm.at[m], train.at[m], train_sem.at[m])

    def each_module(first, last, step):
        def body(m, carry):
            step(m)
            return carry

        lax.fori_loop(first, last, body, 0)

    base = 6 + 2 * FIRST
    load_inner = pltpu.make_async_copy(inner_hbm, inner_ref, basis_sem.at[0])
    load_outer = pltpu.make_async_copy(outer_hbm, outer_ref, basis_sem.at[1])
    load_train(base + core).start()
    load_inner.start()
    load_outer.start()
    load_train(base + 1 - core).start()
    each_module(0, base, lambda m: load_train(m).start())
    each_module(base + 2, MODULES, lambda m: load_train(m).start())

    row, col = iota((256, 256), 0), iota((256, 256), 1)
    swap[...] = one_hot((row // 16 == col % 16) & (row % 16 == col // 16))
    row, col = iota((128, 64), 0), iota((128, 64), 1)
    spread_rows[...] = one_hot(row % 64 == col)
    row, col = iota((64, 256), 0), iota((64, 256), 1)
    spread_lanes[...] = one_hot(col % 64 == row)
    row, col = iota((128, 256), 0), iota((128, 256), 1)
    group = col // 64
    keep[...] = jnp.where(((group == 0) | (group == 3)) == (row < 64), 1.0, 0.0)
    row, col = iota((64, 64), 0), iota((64, 64), 1)
    columns_of[...] = one_hot(col == 2 * (row % 32) + row // 32)
    rows_even[...] = one_hot(row == 2 * (col % 32) + col // 32)
    rows_odd[...] = one_hot(row == 2 * (col % 32) + 1 - col // 32)

    def side_by_side(pieces):
        return jnp.concatenate(pieces, axis=1)

    def stack(pieces):
        return jnp.concatenate(pieces, axis=0)

    def swap_rows(tile):
        pieces = side_by_side([stack([tile(16 * half + c) for c in range(16)]) for half in range(2)])
        return dot(swap[...], pieces).astype(BF16)

    def rotate(*modules):
        for m in modules:
            load_train(m).wait()
        values = [rotation(m) for m in modules]
        for m, value in zip(modules, values):
            rotated[m] = value

    def rotation(m):
        inner = dot(dot(spread_rows[...], inner_ref[m]).astype(BF16), spread_lanes[...])
        inner = (inner * keep[...]).astype(BF16)
        turned = dot_t(columns_of[...], outer_ref[m]).astype(BF16)
        outer = jnp.where(
            iota((64, 64), 0) < 32, dot(turned, rows_even[...]), dot(turned, rows_odd[...])
        ).astype(BF16)
        grads = train[m]
        rows = swap_rows(lambda c: grads[:, c * LANES:(c + 1) * LANES])
        matrices = stack(
            [rows[16 * e:16 * e + 16, h * LANES:(h + 1) * LANES] for e in range(OWN_TRAIN) for h in range(2)]
        )
        half = dot(matrices, inner).astype(BF16)
        stacked = stack(
            [
                side_by_side([half[32 * e:32 * e + 32, h * LANES:(h + 1) * LANES] for e in range(OWN_TRAIN)])
                for h in range(2)
            ]
        )
        both = dot(outer, stacked)
        first = iota((32, OWN_TRAIN * LANES), 1) % LANES < WIDTH
        result = jnp.where(first, both[:32], both[32:]).astype(BF16)
        pieces = side_by_side(
            [
                stack([result[16 * h:16 * h + 16, e * LANES:(e + 1) * LANES] for e in range(OWN_TRAIN)])
                for h in range(2)
            ]
        )
        final = dot(swap[...], pieces).astype(BF16)
        return side_by_side(
            [final[16 * c:16 * c + 16, h * LANES:(h + 1) * LANES] for h in range(2) for c in range(16)]
        )

    def block_copy(slot, partner):
        x, c, device = at_plane(*PARTNERS[partner])
        m = 4 * slot + 2 * x + c if slot < PAIR_SLOTS else 6 + 2 * slot + c
        return pltpu.make_async_remote_copy(
            src_ref=rotated.at[m],
            dst_ref=blocks.at[slot, z, pl.ds(pl.multiple_of(here * 16, 16), 16)],
            send_sem=block_send.at[slot, partner],
            recv_sem=block_recv.at[slot, partner],
            device_id=device,
            device_id_type=MESH,
        )

    def own_copy(slot):
        m = 4 * slot + here if slot < PAIR_SLOTS else 6 + 2 * slot + core
        return pltpu.make_async_copy(
            rotated.at[m], blocks.at[slot, z, pl.ds(pl.multiple_of(here * 16, 16), 16)], local_sem.at[slot]
        )

    def ring_copy(slot, way):
        return pltpu.make_async_remote_copy(
            src_ref=blocks.at[slot, z],
            dst_ref=blocks.at[slot, z],
            send_sem=ring_send.at[slot, way],
            recv_sem=ring_recv.at[slot, way],
            device_id=at_ring(1 - 2 * way),
            device_id_type=MESH,
        )

    def half_copy(slot, way):
        source = (z + DEPTH - 1 + 2 * way) % DEPTH
        half = blocks.at[slot, source, pl.ds(32 * way, 32)]
        return pltpu.make_async_remote_copy(
            src_ref=half,
            dst_ref=half,
            send_sem=half_send.at[slot, way],
            recv_sem=half_recv.at[slot, way],
            device_id=at_ring(1 - 2 * way),
            device_id_type=MESH,
        )

    def query_copy(slot, partner):
        x, c, device = at_plane(*PARTNERS[partner])
        to = pl.ds(pl.multiple_of(PARTNERS[partner][0] * 128 + core * 64, 64), 64)
        if slot < PAIR_SLOTS:
            m, target = 4 * slot + 2 * x + c, pair_queries.at[slot, to]
        else:
            m, target = 6 + 2 * slot + c, column_queries.at[slot - PAIR_SLOTS, to]
        return pltpu.make_async_remote_copy(
            src_ref=query_hbm.at[m],
            dst_ref=target,
            send_sem=query_send.at[slot, partner],
            recv_sem=query_recv.at[slot, partner],
            device_id=device,
            device_id_type=MESH,
        )

    def own_query_copy(slot):
        to = pl.ds(pl.multiple_of(core * 64, 64), 64)
        if slot < PAIR_SLOTS:
            m, target = 4 * slot + here, pair_queries.at[slot, to]
        else:
            m, target = 6 + 2 * slot + core, column_queries.at[slot - PAIR_SLOTS, to]
        return pltpu.make_async_copy(query_hbm.at[m], target, local_query_sem.at[slot])

    def send_blocks(slot):
        for partner in (1, 2, 0):
            block_copy(slot, partner).start()
        own_copy(slot).start()

    def send_ring(slot):
        for partner in range(3):
            block_copy(slot, partner).wait_recv()
        own_copy(slot).wait()
        for way in range(2):
            ring_copy(slot, way).start()

    def send_half(slot):
        for way in range(2):
            ring_copy(slot, way).wait_recv()
            half_copy(slot, way).start()

    def query_partners(slot):
        return (1, 2, 0) if slot < PAIR_SLOTS else (0,)

    def send_queries(slot):
        for partner in query_partners(slot):
            query_copy(slot, partner).start()
        own_query_copy(slot).start()

    def piece_copy(source, way, held=None):
        target = blocks.at[FIRST, z, pl.ds(pl.multiple_of(source * 16, 16), 16)]
        return pltpu.make_async_remote_copy(
            src_ref=target if held is None else held,
            dst_ref=target,
            send_sem=piece_send.at[source, way],
            recv_sem=piece_recv.at[source, way],
            device_id=at_ring(1 - 2 * way),
            device_id_type=MESH,
        )

    def send_own_piece():
        for way in range(2):
            piece_copy(here, way, rotated.at[base + core]).start()
        own_copy(FIRST).start()

    def send_piece(partner):
        block_copy(FIRST, partner).wait_recv()
        x, c, _ = at_plane(*PARTNERS[partner])
        for way in range(2):
            piece_copy(2 * x + c, way).start()

    def send_first_half():
        for way in range(2):
            for source in range(4):
                piece_copy(source, way).wait_recv()
            half_copy(FIRST, way).start()

    def rotate_slot(slot):
        if slot < PAIR_SLOTS:
            each_module(4 * slot, 4 * slot + 4, rotate)
        else:
            each_module(6 + 2 * slot, 8 + 2 * slot, rotate)
        send_blocks(slot)

    load_inner.wait()
    load_outer.wait()
    rotate(base, base + 1)
    rotate(0, 1)
    rotate(2, 3)
    pl.semaphore_wait(barrier, len(PARTNERS) + 2 + 2 * (LAYERS - 1))
    for partner in (0, 1, 2):
        block_copy(FIRST, partner).start()
    send_own_piece()
    send_blocks(0)
    for slot in range(PAIR_SLOTS, SLOTS):
        own_query_copy(slot).start()
        query_copy(slot, 0).start()
    send_piece(0)
    rotate(4, 5)
    send_piece(1)
    send_piece(2)
    rotate(6, 7)
    send_blocks(1)
    send_ring(0)
    rotate(8, 9)
    rotate(10, 11)
    send_blocks(2)
    send_first_half()
    for slot in (4, 5, 6):
        rotate(6 + 2 * slot, 7 + 2 * slot)
        send_blocks(slot)
    send_queries(0)
    send_ring(1)
    own_copy(FIRST).wait()

    def wait_blocks(slot):
        for way in range(2):
            half_copy(slot, way).wait_recv()
        for partner in query_partners(slot):
            query_copy(slot, partner).wait_recv()
        own_query_copy(slot).wait()

    pair_scores[...] = jnp.zeros_like(pair_scores)
    column_scores[...] = jnp.zeros_like(column_scores)

    def score_pair(slot):
        wait_blocks(slot)
        scores = dot_t(blocks[slot].reshape(256, FLAT), pair_queries[slot])
        for side in range(2):
            pair_scores[side] += scores[:, side * LANES:(side + 1) * LANES]

    def score_column(slot):
        wait_blocks(slot)
        column_scores[...] += dot_t(blocks[slot].reshape(256, FLAT), column_queries[slot - PAIR_SLOTS])

    def score_part(step):
        source = (z + step) % DEPTH
        rows = pl.ds(pl.multiple_of(source * 64, 64), 64)
        column_scores[rows, :] += dot_t(blocks[LAST, source], column_queries[LAST - PAIR_SLOTS])

    send_half(0)
    send_ring(2)
    score_column(3)
    send_half(1)
    send_ring(4)
    send_queries(1)
    send_half(2)
    send_ring(5)
    send_queries(2)
    send_half(4)
    send_ring(6)
    score_pair(0)
    send_half(5)
    score_pair(1)
    score_column(4)
    send_half(6)
    score_pair(2)

    cross = pltpu.make_async_remote_copy(
        src_ref=pair_scores.at[1],
        dst_ref=theirs,
        send_sem=pair_send,
        recv_sem=pair_recv,
        device_id=at_plane(1, 0)[2],
        device_id_type=MESH,
    )
    cross.start()
    score_column(5)
    query_copy(LAST, 0).wait_recv()
    own_query_copy(LAST).wait()
    for step in (0, 1, 3):
        score_part(step)
    for way in range(2):
        half_copy(LAST, way).wait_recv()
    score_part(2)
    cross.wait_recv()
    own = pair_scores[0] + column_scores[...] + theirs[...]
    moved = pltpu.roll(own, WIDTH, 1)
    left = iota((LAYERS, 16, LANES), 2) < WIDTH
    own = own.reshape(LAYERS, 2, 16, LANES)
    moved = moved.reshape(LAYERS, 2, 16, LANES)
    packed[:, 0] = jnp.where(left, own[:, 0], moved[:, 1])
    packed[:, 1] = jnp.where(left, moved[:, 0], own[:, 1])

    def layer_copy(step, other):
        return pltpu.make_async_remote_copy(
            src_ref=packed.at[(layer + step) % LAYERS, 1 - core if other else core],
            dst_ref=gathered.at[step, other],
            send_sem=layer_send.at[step, other],
            recv_sem=layer_recv.at[step, other],
            device_id=at_layer(step, other),
            device_id_type=MESH,
        )

    others = [(step, other) for step in range(LAYERS) for other in range(2) if step or other]
    for step, other in others:
        layer_copy(step, other).start()
    total = packed[layer, core]
    for step, other in others:
        layer_copy(step, other).wait_recv()
        total += gathered[step, other]
    out_ref[0:16, :] = total[:, :WIDTH]
    out_ref[16:32, :] = total[:, WIDTH:]

    for step, other in others:
        layer_copy(step, other).wait_send()
    cross.wait_send()
    for slot in range(SLOTS):
        for partner in range(3):
            block_copy(slot, partner).wait_send()
        for partner in query_partners(slot):
            query_copy(slot, partner).wait_send()
        for way in range(2):
            if slot == FIRST:
                for source in range(4):
                    piece_copy(source, way).wait_send()
            else:
                ring_copy(slot, way).wait_send()
            half_copy(slot, way).wait_send()


def shards(train_grads, query_pre, basis_in, basis_out):
    dma = pltpu.SemaphoreType.DMA
    return pl.pallas_call(
        kernel,
        out_shape=jax.ShapeDtypeStruct((32, WIDTH), F32),
        in_specs=[
            pl.BlockSpec(memory_space=pl.ANY),
            pl.BlockSpec(memory_space=pl.ANY),
            pl.BlockSpec(memory_space=pl.ANY),
            pl.BlockSpec(memory_space=pl.ANY),
        ],
        out_specs=pl.BlockSpec(memory_space=pltpu.VMEM),
        scratch_shapes=[
            pltpu.VMEM((MODULES, WIDTH, WIDTH), BF16),
            pltpu.VMEM((MODULES, WIDTH, WIDTH), BF16),
            pltpu.VMEM((MODULES, OWN_TRAIN, FLAT), BF16),
            pltpu.VMEM((MODULES, OWN_TRAIN, FLAT), BF16),
            pltpu.VMEM((SLOTS, DEPTH, 64, FLAT), BF16),
            pltpu.VMEM((PAIR_SLOTS, 256, FLAT), BF16),
            pltpu.VMEM((COLUMN_SLOTS, 128, FLAT), BF16),
            pltpu.VMEM((256, 256), BF16),
            pltpu.VMEM((128, 64), BF16),
            pltpu.VMEM((64, 256), BF16),
            pltpu.VMEM((128, 256), F32),
            pltpu.VMEM((64, 64), BF16),
            pltpu.VMEM((64, 64), BF16),
            pltpu.VMEM((64, 64), BF16),
            pltpu.VMEM((2, 256, LANES), F32),
            pltpu.VMEM((256, LANES), F32),
            pltpu.VMEM((256, LANES), F32),
            pltpu.VMEM((LAYERS, 2, 16, LANES), F32),
            pltpu.VMEM((LAYERS, 2, 16, LANES), F32),
            dma((2,)), dma((MODULES,)), dma((SLOTS,)), dma((SLOTS,)),
            dma((SLOTS, 3)), dma((SLOTS, 3)), dma((4, 2)), dma((4, 2)), dma((SLOTS, 2)), dma((SLOTS, 2)), dma((SLOTS, 2)), dma((SLOTS, 2)),
            dma((SLOTS, 3)), dma((SLOTS, 3)), dma, dma, dma((LAYERS, 2)), dma((LAYERS, 2)),
        ],
        compiler_params=pltpu.CompilerParams(
            collective_id=0, has_side_effects=True, vmem_limit_bytes=62 * 2**20
        ),
        name="influence_scores",
    )(jnp.transpose(train_grads, (1, 0, 2)), jnp.transpose(query_pre, (1, 0, 2)), basis_in, basis_out)


def solution(mesh):
    placed = (
        P("query", "layer", None),
        P("query", "layer", None),
        P("layer", None, None),
        P("layer", None, None),
    )
    return jax.shard_map(
        shards, mesh=mesh, in_specs=placed, out_specs=P("layer", "query"), check_vma=False
    )
```

```python
import jax
import jax.numpy as jnp
from jax import lax
from jax.experimental import pallas as pl
from jax.experimental.pallas import tpu as pltpu
from jax.sharding import PartitionSpec as P

MESH = pl.DeviceIdType.MESH
BF16 = jnp.bfloat16
F32 = jnp.float32

WIDTH = 64
FLAT = WIDTH * WIDTH
MODULES = 20
OWN_TRAIN = 16
LAYERS = 8
DEPTH = 4
SLOTS = 8
FIRST = 3
LAST = 6
EXTRA = 7
SHARED = 1024
REST = FLAT - SHARED
IN_PIECES = (FIRST, 0)
LANES = 128
PARTNERS = ((0, 1), (1, 0), (1, 1))


def dot(a, b):
    return jnp.dot(a, b, preferred_element_type=F32)


def dot_t(a, b):
    return lax.dot_general(a, b, (((1,), (1,)), ((), ())), preferred_element_type=F32)


def iota(shape, dim):
    return lax.broadcasted_iota(jnp.int32, shape, dim)


def one_hot(condition):
    return jnp.where(condition, 1.0, 0.0).astype(BF16)


def kernel(
    train_hbm, query_hbm, inner_hbm, outer_hbm, out_ref,
    inner_ref, outer_ref,
    train, rotated, full_blocks, rest_blocks, extra_blocks, pair_queries, extra_queries, column_queries, rest_queries,
    swap, spread_rows, spread_lanes, keep, columns_of, rows_even, rows_odd,
    pair_scores, column_scores, theirs, packed, gathered,
    basis_sem, train_sem, local_sem, local_query_sem,
    block_send, block_recv, piece_send, piece_recv, ring_send, ring_recv, half_send, half_recv,
    query_send, query_recv, pair_send, pair_recv, layer_send, layer_recv,
):
    layer = lax.axis_index("layer")
    place = lax.axis_index("query")
    z = place // 4
    column = (place // 2) % 2
    core = place % 2
    here = place % 4

    def at_plane(other_column, other_core):
        x = 1 - column if other_column else column
        c = 1 - core if other_core else core
        return x, c, (layer, z * 4 + x * 2 + c)

    def at_ring(step):
        return (layer, ((z + step + DEPTH) % DEPTH) * 4 + here)

    def at_layer(step, other_core):
        c = 1 - core if other_core else core
        return ((layer + step) % LAYERS, z * 4 + column * 2 + c)

    barrier = pltpu.get_barrier_semaphore()
    for partner in PARTNERS:
        pl.semaphore_signal(barrier, inc=1, device_id=at_plane(*partner)[2], device_id_type=MESH)
    for step in (1, -1):
        pl.semaphore_signal(barrier, inc=1, device_id=at_ring(step), device_id_type=MESH)
    for step in range(1, LAYERS):
        for other in range(2):
            pl.semaphore_signal(barrier, inc=1, device_id=at_layer(step, other), device_id_type=MESH)

    def load_train(m):
        return pltpu.make_async_copy(train_hbm.at[m], train.at[m], train_sem.at[m])

    def each_module(first, last, step):
        def body(m, carry):
            step(m)
            return carry

        lax.fori_loop(first, last, body, 0)

    base = 6 + 2 * FIRST
    load_inner = pltpu.make_async_copy(inner_hbm, inner_ref, basis_sem.at[0])
    load_outer = pltpu.make_async_copy(outer_hbm, outer_ref, basis_sem.at[1])
    load_train(base + core).start()
    load_inner.start()
    load_outer.start()
    load_train(base + 1 - core).start()
    each_module(0, base, lambda m: load_train(m).start())
    each_module(base + 2, MODULES, lambda m: load_train(m).start())

    row, col = iota((256, 256), 0), iota((256, 256), 1)
    swap[...] = one_hot((row // 16 == col % 16) & (row % 16 == col // 16))
    row, col = iota((128, 64), 0), iota((128, 64), 1)
    spread_rows[...] = one_hot(row % 64 == col)
    row, col = iota((64, 256), 0), iota((64, 256), 1)
    spread_lanes[...] = one_hot(col % 64 == row)
    row, col = iota((128, 256), 0), iota((128, 256), 1)
    group = col // 64
    keep[...] = jnp.where(((group == 0) | (group == 3)) == (row < 64), 1.0, 0.0)
    row, col = iota((64, 64), 0), iota((64, 64), 1)
    columns_of[...] = one_hot(col == 2 * (row % 32) + row // 32)
    rows_even[...] = one_hot(row == 2 * (col % 32) + col // 32)
    rows_odd[...] = one_hot(row == 2 * (col % 32) + 1 - col // 32)

    def side_by_side(pieces):
        return jnp.concatenate(pieces, axis=1)

    def stack(pieces):
        return jnp.concatenate(pieces, axis=0)

    def swap_rows(tile):
        pieces = side_by_side([stack([tile(16 * half + c) for c in range(16)]) for half in range(2)])
        return dot(swap[...], pieces).astype(BF16)

    def rotate(*modules):
        for m in modules:
            load_train(m).wait()
        values = [rotation(m) for m in modules]
        for m, value in zip(modules, values):
            rotated[m] = value

    def rotation(m):
        inner = dot(dot(spread_rows[...], inner_ref[m]).astype(BF16), spread_lanes[...])
        inner = (inner * keep[...]).astype(BF16)
        turned = dot_t(columns_of[...], outer_ref[m]).astype(BF16)
        outer = jnp.where(
            iota((64, 64), 0) < 32, dot(turned, rows_even[...]), dot(turned, rows_odd[...])
        ).astype(BF16)
        grads = train[m]
        rows = swap_rows(lambda c: grads[:, c * LANES:(c + 1) * LANES])
        matrices = stack(
            [rows[16 * e:16 * e + 16, h * LANES:(h + 1) * LANES] for e in range(OWN_TRAIN) for h in range(2)]
        )
        half = dot(matrices, inner).astype(BF16)
        stacked = stack(
            [
                side_by_side([half[32 * e:32 * e + 32, h * LANES:(h + 1) * LANES] for e in range(OWN_TRAIN)])
                for h in range(2)
            ]
        )
        both = dot(outer, stacked)
        first = iota((32, OWN_TRAIN * LANES), 1) % LANES < WIDTH
        result = jnp.where(first, both[:32], both[32:]).astype(BF16)
        pieces = side_by_side(
            [
                stack([result[16 * h:16 * h + 16, e * LANES:(e + 1) * LANES] for e in range(OWN_TRAIN)])
                for h in range(2)
            ]
        )
        final = dot(swap[...], pieces).astype(BF16)
        return side_by_side(
            [final[16 * c:16 * c + 16, h * LANES:(h + 1) * LANES] for h in range(2) for c in range(16)]
        )

    def is_pair(slot):
        return slot < 3 or slot == EXTRA

    def module_of(slot, x, c):
        if slot == EXTRA:
            return 16 + 2 * x + c
        return 4 * slot + 2 * x + c if is_pair(slot) else 6 + 2 * slot + c

    def entries(slot):
        if slot == EXTRA:
            return pl.ds(0, SHARED)
        return pl.ds(SHARED, REST) if slot >= 5 else pl.ds(0, FLAT)

    def blocks(slot):
        if slot == EXTRA:
            return extra_blocks
        return rest_blocks.at[slot - 5] if slot >= 5 else full_blocks.at[slot]

    def queries(slot):
        if is_pair(slot):
            return extra_queries if slot == EXTRA else pair_queries.at[slot]
        return rest_queries.at[slot - 5] if slot >= 5 else column_queries.at[slot - 3]

    def own_rows(count, first):
        return pl.ds(pl.multiple_of(first * count, count), count)

    def block_copy(slot, partner):
        x, c, device = at_plane(*PARTNERS[partner])
        return pltpu.make_async_remote_copy(
            src_ref=rotated.at[module_of(slot, x, c), :, entries(slot)],
            dst_ref=blocks(slot).at[z, own_rows(16, here)],
            send_sem=block_send.at[slot, partner],
            recv_sem=block_recv.at[slot, partner],
            device_id=device,
            device_id_type=MESH,
        )

    def own_copy(slot):
        return pltpu.make_async_copy(
            rotated.at[module_of(slot, column, core), :, entries(slot)],
            blocks(slot).at[z, own_rows(16, here)],
            local_sem.at[slot],
        )

    def ring_copy(slot, way):
        return pltpu.make_async_remote_copy(
            src_ref=blocks(slot).at[z],
            dst_ref=blocks(slot).at[z],
            send_sem=ring_send.at[slot, way],
            recv_sem=ring_recv.at[slot, way],
            device_id=at_ring(1 - 2 * way),
            device_id_type=MESH,
        )

    def half_copy(slot, way):
        source = (z + DEPTH - 1 + 2 * way) % DEPTH
        half = blocks(slot).at[source, pl.ds(32 * way, 32)]
        return pltpu.make_async_remote_copy(
            src_ref=half,
            dst_ref=half,
            send_sem=half_send.at[slot, way],
            recv_sem=half_recv.at[slot, way],
            device_id=at_ring(1 - 2 * way),
            device_id_type=MESH,
        )

    def query_copy(slot, partner):
        x, c, device = at_plane(*PARTNERS[partner])
        return pltpu.make_async_remote_copy(
            src_ref=query_hbm.at[module_of(slot, x, c), :, entries(slot)],
            dst_ref=queries(slot).at[own_rows(64, PARTNERS[partner][0] * 2 + core)],
            send_sem=query_send.at[slot, partner],
            recv_sem=query_recv.at[slot, partner],
            device_id=device,
            device_id_type=MESH,
        )

    def own_query_copy(slot):
        return pltpu.make_async_copy(
            query_hbm.at[module_of(slot, column, core), :, entries(slot)],
            queries(slot).at[own_rows(64, core)],
            local_query_sem.at[slot],
        )

    def piece_copy(slot, source, way, held=None):
        target = blocks(slot).at[z, own_rows(16, source)]
        return pltpu.make_async_remote_copy(
            src_ref=target if held is None else held,
            dst_ref=target,
            send_sem=piece_send.at[IN_PIECES.index(slot), source, way],
            recv_sem=piece_recv.at[IN_PIECES.index(slot), source, way],
            device_id=at_ring(1 - 2 * way),
            device_id_type=MESH,
        )

    def query_partners(slot):
        return (1, 2, 0) if is_pair(slot) else (0,)

    def send_queries(slot):
        for partner in query_partners(slot):
            query_copy(slot, partner).start()
        own_query_copy(slot).start()

    def send_blocks(slot):
        for partner in (1, 2, 0):
            block_copy(slot, partner).start()
        if slot in IN_PIECES:
            for way in range(2):
                piece_copy(slot, here, way, rotated.at[module_of(slot, column, core)]).start()
        own_copy(slot).start()

    def send_piece(slot, partner):
        block_copy(slot, partner).wait_recv()
        x, c, _ = at_plane(*PARTNERS[partner])
        for way in range(2):
            piece_copy(slot, 2 * x + c, way).start()

    def send_ring(slot):
        for partner in range(3):
            block_copy(slot, partner).wait_recv()
        own_copy(slot).wait()
        for way in range(2):
            ring_copy(slot, way).start()

    def send_half(slot):
        for way in range(2):
            if slot in IN_PIECES:
                for source in range(4):
                    piece_copy(slot, source, way).wait_recv()
            else:
                ring_copy(slot, way).wait_recv()
            half_copy(slot, way).start()

    load_inner.wait()
    load_outer.wait()
    rotate(base, base + 1)
    pl.semaphore_wait(barrier, len(PARTNERS) + 2 + 2 * (LAYERS - 1))
    send_blocks(3)
    rotate(0, 1)
    send_piece(3, 0)
    rotate(2, 3)
    send_blocks(0)
    send_piece(3, 1)
    rotate(4, 5)
    send_piece(3, 2)
    send_piece(0, 0)
    rotate(6, 7)
    send_blocks(1)
    send_piece(0, 1)
    rotate(8, 9)
    send_piece(0, 2)
    rotate(10, 11)
    send_blocks(2)
    for slot in (3, 4, 5, 6):
        send_queries(slot)
    send_half(3)
    rotate(16, 17)
    rotate(18, 19)
    send_blocks(7)
    rotate(14, 15)
    send_blocks(4)
    send_blocks(5)
    send_blocks(6)
    send_queries(0)
    send_ring(1)

    def wait_blocks(slot):
        for way in range(2):
            half_copy(slot, way).wait_recv()
        if slot in IN_PIECES:
            own_copy(slot).wait()
        wait_queries(slot)

    def wait_queries(slot):
        for partner in query_partners(slot):
            query_copy(slot, partner).wait_recv()
        own_query_copy(slot).wait()

    pair_scores[...] = jnp.zeros_like(pair_scores)
    column_scores[...] = jnp.zeros_like(column_scores)

    def score(slot):
        wait_blocks(slot)
        rows = blocks(slot)[...]
        scores = dot_t(rows.reshape(256, rows.shape[2]), queries(slot)[...])
        if is_pair(slot):
            for side in range(2):
                pair_scores[side] += scores[:, side * LANES:(side + 1) * LANES]
        else:
            column_scores[...] += scores

    def score_part(step):
        source = (z + step) % DEPTH
        rows = pl.ds(pl.multiple_of(source * 64, 64), 64)
        column_scores[rows, :] += dot_t(blocks(LAST)[source], queries(LAST)[...])

    send_half(0)
    send_ring(2)
    score(3)
    send_half(1)
    send_ring(7)
    send_queries(1)
    send_queries(7)
    send_half(2)
    send_ring(4)
    send_queries(2)
    send_half(7)
    send_ring(5)
    score(0)
    send_half(4)
    send_ring(6)
    score(1)
    send_half(5)
    score(4)
    score(7)
    send_half(6)
    score(2)

    cross = pltpu.make_async_remote_copy(
        src_ref=pair_scores.at[1],
        dst_ref=theirs,
        send_sem=pair_send,
        recv_sem=pair_recv,
        device_id=at_plane(1, 0)[2],
        device_id_type=MESH,
    )
    cross.start()
    score(5)
    wait_queries(LAST)
    for step in (0, 1, 3):
        score_part(step)
    for way in range(2):
        half_copy(LAST, way).wait_recv()
    score_part(2)
    cross.wait_recv()
    own = pair_scores[0] + column_scores[...] + theirs[...]
    moved = pltpu.roll(own, WIDTH, 1)
    left = iota((LAYERS, 16, LANES), 2) < WIDTH
    own = own.reshape(LAYERS, 2, 16, LANES)
    moved = moved.reshape(LAYERS, 2, 16, LANES)
    packed[:, 0] = jnp.where(left, own[:, 0], moved[:, 1])
    packed[:, 1] = jnp.where(left, moved[:, 0], own[:, 1])

    def layer_copy(step, other):
        return pltpu.make_async_remote_copy(
            src_ref=packed.at[(layer + step) % LAYERS, 1 - core if other else core],
            dst_ref=gathered.at[step, other],
            send_sem=layer_send.at[step, other],
            recv_sem=layer_recv.at[step, other],
            device_id=at_layer(step, other),
            device_id_type=MESH,
        )

    others = [(step, other) for step in range(LAYERS) for other in range(2) if step or other]
    for step, other in others:
        layer_copy(step, other).start()
    total = packed[layer, core]
    for step, other in others:
        layer_copy(step, other).wait_recv()
        total += gathered[step, other]
    out_ref[0:16, :] = total[:, :WIDTH]
    out_ref[16:32, :] = total[:, WIDTH:]

    for step, other in others:
        layer_copy(step, other).wait_send()
    cross.wait_send()
    for slot in range(SLOTS):
        for partner in range(3):
            block_copy(slot, partner).wait_send()
        for partner in query_partners(slot):
            query_copy(slot, partner).wait_send()
        for way in range(2):
            if slot in IN_PIECES:
                for source in range(4):
                    piece_copy(slot, source, way).wait_send()
            else:
                ring_copy(slot, way).wait_send()
            half_copy(slot, way).wait_send()


def shards(train_grads, query_pre, basis_in, basis_out):
    dma = pltpu.SemaphoreType.DMA
    return pl.pallas_call(
        kernel,
        out_shape=jax.ShapeDtypeStruct((32, WIDTH), F32),
        in_specs=[
            pl.BlockSpec(memory_space=pl.ANY),
            pl.BlockSpec(memory_space=pl.ANY),
            pl.BlockSpec(memory_space=pl.ANY),
            pl.BlockSpec(memory_space=pl.ANY),
        ],
        out_specs=pl.BlockSpec(memory_space=pltpu.VMEM),
        scratch_shapes=[
            pltpu.VMEM((MODULES, WIDTH, WIDTH), BF16),
            pltpu.VMEM((MODULES, WIDTH, WIDTH), BF16),
            pltpu.VMEM((MODULES, OWN_TRAIN, FLAT), BF16),
            pltpu.VMEM((MODULES, OWN_TRAIN, FLAT), BF16),
            pltpu.VMEM((5, DEPTH, 64, FLAT), BF16),
            pltpu.VMEM((2, DEPTH, 64, REST), BF16),
            pltpu.VMEM((DEPTH, 64, SHARED), BF16),
            pltpu.VMEM((3, 256, FLAT), BF16),
            pltpu.VMEM((256, SHARED), BF16),
            pltpu.VMEM((2, 128, FLAT), BF16),
            pltpu.VMEM((2, 128, REST), BF16),
            pltpu.VMEM((256, 256), BF16),
            pltpu.VMEM((128, 64), BF16),
            pltpu.VMEM((64, 256), BF16),
            pltpu.VMEM((128, 256), F32),
            pltpu.VMEM((64, 64), BF16),
            pltpu.VMEM((64, 64), BF16),
            pltpu.VMEM((64, 64), BF16),
            pltpu.VMEM((2, 256, LANES), F32),
            pltpu.VMEM((256, LANES), F32),
            pltpu.VMEM((256, LANES), F32),
            pltpu.VMEM((LAYERS, 2, 16, LANES), F32),
            pltpu.VMEM((LAYERS, 2, 16, LANES), F32),
            dma((2,)), dma((MODULES,)), dma((SLOTS,)), dma((SLOTS,)),
            dma((SLOTS, 3)), dma((SLOTS, 3)), dma((2, 4, 2)), dma((2, 4, 2)), dma((SLOTS, 2)), dma((SLOTS, 2)), dma((SLOTS, 2)), dma((SLOTS, 2)),
            dma((SLOTS, 3)), dma((SLOTS, 3)), dma, dma, dma((LAYERS, 2)), dma((LAYERS, 2)),
        ],
        compiler_params=pltpu.CompilerParams(
            collective_id=0, has_side_effects=True, vmem_limit_bytes=62 * 2**20
        ),
        name="influence_scores",
    )(jnp.transpose(train_grads, (1, 0, 2)), jnp.transpose(query_pre, (1, 0, 2)), basis_in, basis_out)


def solution(mesh):
    placed = (
        P("query", "layer", None),
        P("query", "layer", None),
        P("layer", None, None),
        P("layer", None, None),
    )
    return jax.shard_map(
        shards, mesh=mesh, in_specs=placed, out_specs=P("layer", "query"), check_vma=False
    )
```

```python
import jax
import jax.numpy as jnp
from jax import lax
from jax.experimental import pallas as pl
from jax.experimental.pallas import tpu as pltpu
from jax.sharding import PartitionSpec as P

MESH = pl.DeviceIdType.MESH
BF16 = jnp.bfloat16
F32 = jnp.float32

WIDTH = 64
FLAT = WIDTH * WIDTH
MODULES = 20
OWN_TRAIN = 16
LAYERS = 8
DEPTH = 4
SLOTS = 8
FIRST = 3
LAST = 6
EXTRA = 7
SHARED = 1024
REST = FLAT - SHARED
IN_PIECES = (FIRST, 0)
FAR_FIRST = ((1, 2), (1, 1), (1, 3), (0, 2), (1, 0), (0, 1), (0, 3), (0, 0))
LANES = 128
PARTNERS = ((0, 1), (1, 0), (1, 1))


def dot(a, b):
    return jnp.dot(a, b, preferred_element_type=F32)


def dot_t(a, b):
    return lax.dot_general(a, b, (((1,), (1,)), ((), ())), preferred_element_type=F32)


def iota(shape, dim):
    return lax.broadcasted_iota(jnp.int32, shape, dim)


def one_hot(condition):
    return jnp.where(condition, 1.0, 0.0).astype(BF16)


def kernel(
    train_hbm, query_hbm, inner_hbm, outer_hbm, out_ref,
    inner_ref, outer_ref,
    train, rotated, full_blocks, rest_blocks, extra_blocks, pair_queries, extra_queries, column_queries, rest_queries,
    swap, spread_rows, spread_lanes, keep, columns_of, rows_even, rows_odd,
    pair_scores, column_scores, theirs, packed, gathered,
    basis_sem, train_sem, local_sem, local_query_sem,
    block_send, block_recv, piece_send, piece_recv, ring_send, ring_recv, half_send, half_recv,
    query_send, query_recv, pair_send, pair_recv, layer_send, layer_recv, told,
):
    layer = lax.axis_index("layer")
    place = lax.axis_index("query")
    z = place // 4
    column = (place // 2) % 2
    core = place % 2
    here = place % 4

    def at_plane(other_column, other_core):
        x = 1 - column if other_column else column
        c = 1 - core if other_core else core
        return x, c, (layer, z * 4 + x * 2 + c)

    def at_ring(step):
        return (layer, ((z + step + DEPTH) % DEPTH) * 4 + here)

    def layer_at(over, step):
        return (layer // 4 + over) % 2 * 4 + (layer + step) % 4

    def at_layer(over, step, other_core):
        c = 1 - core if other_core else core
        return (layer_at(over, step), z * 4 + column * 2 + c)

    near = (at_layer(0, 1, 0), at_layer(0, 3, 0), at_layer(1, 0, 0), at_layer(0, 0, 1))

    def tell(turn):
        for device in near:
            pl.semaphore_signal(told.at[turn], inc=1, device_id=device, device_id_type=MESH)

    def hear(turn):
        pl.semaphore_wait(told.at[turn], len(near))

    barrier = pltpu.get_barrier_semaphore()
    for partner in PARTNERS:
        pl.semaphore_signal(barrier, inc=1, device_id=at_plane(*partner)[2], device_id_type=MESH)
    for step in (1, -1):
        pl.semaphore_signal(barrier, inc=1, device_id=at_ring(step), device_id_type=MESH)
    for device in near[:3]:
        pl.semaphore_signal(barrier, inc=1, device_id=device, device_id_type=MESH)

    def load_train(m):
        return pltpu.make_async_copy(train_hbm.at[m], train.at[m], train_sem.at[m])

    def each_module(first, last, step):
        def body(m, carry):
            step(m)
            return carry

        lax.fori_loop(first, last, body, 0)

    base = 6 + 2 * FIRST
    load_inner = pltpu.make_async_copy(inner_hbm, inner_ref, basis_sem.at[0])
    load_outer = pltpu.make_async_copy(outer_hbm, outer_ref, basis_sem.at[1])
    load_train(base + core).start()
    load_inner.start()
    load_outer.start()
    load_train(base + 1 - core).start()
    each_module(0, base, lambda m: load_train(m).start())
    each_module(base + 2, MODULES, lambda m: load_train(m).start())

    row, col = iota((256, 256), 0), iota((256, 256), 1)
    swap[...] = one_hot((row // 16 == col % 16) & (row % 16 == col // 16))
    row, col = iota((128, 64), 0), iota((128, 64), 1)
    spread_rows[...] = one_hot(row % 64 == col)
    row, col = iota((64, 256), 0), iota((64, 256), 1)
    spread_lanes[...] = one_hot(col % 64 == row)
    row, col = iota((128, 256), 0), iota((128, 256), 1)
    group = col // 64
    keep[...] = jnp.where(((group == 0) | (group == 3)) == (row < 64), 1.0, 0.0)
    row, col = iota((64, 64), 0), iota((64, 64), 1)
    columns_of[...] = one_hot(col == 2 * (row % 32) + row // 32)
    rows_even[...] = one_hot(row == 2 * (col % 32) + col // 32)
    rows_odd[...] = one_hot(row == 2 * (col % 32) + 1 - col // 32)

    def side_by_side(pieces):
        return jnp.concatenate(pieces, axis=1)

    def stack(pieces):
        return jnp.concatenate(pieces, axis=0)

    def swap_rows(tile):
        pieces = side_by_side([stack([tile(16 * half + c) for c in range(16)]) for half in range(2)])
        return dot(swap[...], pieces).astype(BF16)

    def rotate(*modules):
        for m in modules:
            load_train(m).wait()
        values = [rotation(m) for m in modules]
        for m, value in zip(modules, values):
            rotated[m] = value

    def rotation(m):
        inner = dot(dot(spread_rows[...], inner_ref[m]).astype(BF16), spread_lanes[...])
        inner = (inner * keep[...]).astype(BF16)
        turned = dot_t(columns_of[...], outer_ref[m]).astype(BF16)
        outer = jnp.where(
            iota((64, 64), 0) < 32, dot(turned, rows_even[...]), dot(turned, rows_odd[...])
        ).astype(BF16)
        grads = train[m]
        rows = swap_rows(lambda c: grads[:, c * LANES:(c + 1) * LANES])
        matrices = stack(
            [rows[16 * e:16 * e + 16, h * LANES:(h + 1) * LANES] for e in range(OWN_TRAIN) for h in range(2)]
        )
        half = dot(matrices, inner).astype(BF16)
        stacked = stack(
            [
                side_by_side([half[32 * e:32 * e + 32, h * LANES:(h + 1) * LANES] for e in range(OWN_TRAIN)])
                for h in range(2)
            ]
        )
        both = dot(outer, stacked)
        first = iota((32, OWN_TRAIN * LANES), 1) % LANES < WIDTH
        result = jnp.where(first, both[:32], both[32:]).astype(BF16)
        pieces = side_by_side(
            [
                stack([result[16 * h:16 * h + 16, e * LANES:(e + 1) * LANES] for e in range(OWN_TRAIN)])
                for h in range(2)
            ]
        )
        final = dot(swap[...], pieces).astype(BF16)
        return side_by_side(
            [final[16 * c:16 * c + 16, h * LANES:(h + 1) * LANES] for h in range(2) for c in range(16)]
        )

    def is_pair(slot):
        return slot < 3 or slot == EXTRA

    def module_of(slot, x, c):
        if slot == EXTRA:
            return 16 + 2 * x + c
        return 4 * slot + 2 * x + c if is_pair(slot) else 6 + 2 * slot + c

    def entries(slot):
        if slot == EXTRA:
            return pl.ds(0, SHARED)
        return pl.ds(SHARED, REST) if slot >= 5 else pl.ds(0, FLAT)

    def blocks(slot):
        if slot == EXTRA:
            return extra_blocks
        return rest_blocks.at[slot - 5] if slot >= 5 else full_blocks.at[slot]

    def queries(slot):
        if is_pair(slot):
            return extra_queries if slot == EXTRA else pair_queries.at[slot]
        return rest_queries.at[slot - 5] if slot >= 5 else column_queries.at[slot - 3]

    def own_rows(count, first):
        return pl.ds(pl.multiple_of(first * count, count), count)

    def block_copy(slot, partner):
        x, c, device = at_plane(*PARTNERS[partner])
        return pltpu.make_async_remote_copy(
            src_ref=rotated.at[module_of(slot, x, c), :, entries(slot)],
            dst_ref=blocks(slot).at[z, own_rows(16, here)],
            send_sem=block_send.at[slot, partner],
            recv_sem=block_recv.at[slot, partner],
            device_id=device,
            device_id_type=MESH,
        )

    def own_copy(slot):
        return pltpu.make_async_copy(
            rotated.at[module_of(slot, column, core), :, entries(slot)],
            blocks(slot).at[z, own_rows(16, here)],
            local_sem.at[slot],
        )

    def ring_copy(slot, way):
        return pltpu.make_async_remote_copy(
            src_ref=blocks(slot).at[z],
            dst_ref=blocks(slot).at[z],
            send_sem=ring_send.at[slot, way],
            recv_sem=ring_recv.at[slot, way],
            device_id=at_ring(1 - 2 * way),
            device_id_type=MESH,
        )

    def half_copy(slot, way):
        source = (z + DEPTH - 1 + 2 * way) % DEPTH
        half = blocks(slot).at[source, pl.ds(32 * way, 32)]
        return pltpu.make_async_remote_copy(
            src_ref=half,
            dst_ref=half,
            send_sem=half_send.at[slot, way],
            recv_sem=half_recv.at[slot, way],
            device_id=at_ring(1 - 2 * way),
            device_id_type=MESH,
        )

    def query_copy(slot, partner):
        x, c, device = at_plane(*PARTNERS[partner])
        return pltpu.make_async_remote_copy(
            src_ref=query_hbm.at[module_of(slot, x, c), :, entries(slot)],
            dst_ref=queries(slot).at[own_rows(64, PARTNERS[partner][0] * 2 + core)],
            send_sem=query_send.at[slot, partner],
            recv_sem=query_recv.at[slot, partner],
            device_id=device,
            device_id_type=MESH,
        )

    def own_query_copy(slot):
        return pltpu.make_async_copy(
            query_hbm.at[module_of(slot, column, core), :, entries(slot)],
            queries(slot).at[own_rows(64, core)],
            local_query_sem.at[slot],
        )

    def piece_copy(slot, source, way, held=None):
        target = blocks(slot).at[z, own_rows(16, source)]
        return pltpu.make_async_remote_copy(
            src_ref=target if held is None else held,
            dst_ref=target,
            send_sem=piece_send.at[IN_PIECES.index(slot), source, way],
            recv_sem=piece_recv.at[IN_PIECES.index(slot), source, way],
            device_id=at_ring(1 - 2 * way),
            device_id_type=MESH,
        )

    def query_partners(slot):
        return (1, 2, 0) if is_pair(slot) else (0,)

    def send_queries(slot):
        for partner in query_partners(slot):
            query_copy(slot, partner).start()
        own_query_copy(slot).start()

    def send_blocks(slot):
        for partner in (1, 2, 0):
            block_copy(slot, partner).start()
        if slot in IN_PIECES:
            for way in range(2):
                piece_copy(slot, here, way, rotated.at[module_of(slot, column, core)]).start()
        own_copy(slot).start()

    def send_piece(slot, partner):
        block_copy(slot, partner).wait_recv()
        x, c, _ = at_plane(*PARTNERS[partner])
        for way in range(2):
            piece_copy(slot, 2 * x + c, way).start()

    def send_ring(slot):
        for partner in range(3):
            block_copy(slot, partner).wait_recv()
        own_copy(slot).wait()
        for way in range(2):
            ring_copy(slot, way).start()

    def send_half(slot):
        for way in range(2):
            if slot in IN_PIECES:
                for source in range(4):
                    piece_copy(slot, source, way).wait_recv()
            else:
                ring_copy(slot, way).wait_recv()
            half_copy(slot, way).start()

    load_inner.wait()
    load_outer.wait()
    rotate(base, base + 1)
    pl.semaphore_wait(barrier, len(PARTNERS) + 2 + 3)
    send_blocks(3)
    tell(0)
    rotate(0, 1)
    send_piece(3, 0)
    rotate(2, 3)
    send_blocks(0)
    send_piece(3, 1)
    rotate(4, 5)
    send_piece(3, 2)
    send_piece(0, 0)
    rotate(6, 7)
    send_blocks(1)
    send_piece(0, 1)
    rotate(8, 9)
    send_piece(0, 2)
    rotate(10, 11)
    send_blocks(2)
    hear(0)
    tell(1)
    for slot in (3, 4, 5, 6):
        send_queries(slot)
    send_half(3)
    rotate(16, 17)
    rotate(18, 19)
    send_blocks(7)
    rotate(14, 15)
    send_blocks(4)
    send_blocks(5)
    send_blocks(6)
    send_queries(0)
    send_ring(1)
    hear(1)
    tell(2)

    def wait_blocks(slot):
        for way in range(2):
            half_copy(slot, way).wait_recv()
        if slot in IN_PIECES:
            own_copy(slot).wait()
        wait_queries(slot)

    def wait_queries(slot):
        for partner in query_partners(slot):
            query_copy(slot, partner).wait_recv()
        own_query_copy(slot).wait()

    pair_scores[...] = jnp.zeros_like(pair_scores)
    column_scores[...] = jnp.zeros_like(column_scores)

    def score(slot):
        wait_blocks(slot)
        rows = blocks(slot)[...]
        scores = dot_t(rows.reshape(256, rows.shape[2]), queries(slot)[...])
        if is_pair(slot):
            for side in range(2):
                pair_scores[side] += scores[:, side * LANES:(side + 1) * LANES]
        else:
            column_scores[...] += scores

    def score_part(step):
        source = (z + step) % DEPTH
        rows = pl.ds(pl.multiple_of(source * 64, 64), 64)
        column_scores[rows, :] += dot_t(blocks(LAST)[source], queries(LAST)[...])

    send_ring(2)
    send_half(0)
    send_ring(7)
    send_half(1)
    send_ring(4)
    send_queries(1)
    send_queries(7)
    score(3)
    hear(2)
    send_half(2)
    send_ring(5)
    send_queries(2)
    send_half(7)
    send_ring(6)
    send_half(4)
    score(0)
    score(1)
    send_half(5)
    score(4)
    score(7)
    send_half(6)
    score(2)

    cross = pltpu.make_async_remote_copy(
        src_ref=pair_scores.at[1],
        dst_ref=theirs,
        send_sem=pair_send,
        recv_sem=pair_recv,
        device_id=at_plane(1, 0)[2],
        device_id_type=MESH,
    )
    cross.start()
    score(5)
    wait_queries(LAST)
    for step in (0, 1, 3):
        score_part(step)
    for way in range(2):
        half_copy(LAST, way).wait_recv()
    score_part(2)
    cross.wait_recv()
    own = pair_scores[0] + column_scores[...] + theirs[...]
    moved = pltpu.roll(own, WIDTH, 1)
    left = iota((LAYERS, 16, LANES), 2) < WIDTH
    own = own.reshape(LAYERS, 2, 16, LANES)
    moved = moved.reshape(LAYERS, 2, 16, LANES)
    packed[:, 0] = jnp.where(left, own[:, 0], moved[:, 1])
    packed[:, 1] = jnp.where(left, moved[:, 0], own[:, 1])

    def layer_copy(over, step, other):
        return pltpu.make_async_remote_copy(
            src_ref=packed.at[layer_at(over, step), 1 - core if other else core],
            dst_ref=gathered.at[over * 4 + step, other],
            send_sem=layer_send.at[over * 4 + step, other],
            recv_sem=layer_recv.at[over * 4 + step, other],
            device_id=at_layer(over, step, other),
            device_id_type=MESH,
        )

    others = [(over, step, other) for over, step in FAR_FIRST for other in (1, 0) if over or step or other]
    for each in others:
        layer_copy(*each).start()
    for each in others:
        layer_copy(*each).wait_send()
    cross.wait_send()
    for slot in range(SLOTS):
        for partner in range(3):
            block_copy(slot, partner).wait_send()
        for partner in query_partners(slot):
            query_copy(slot, partner).wait_send()
        for way in range(2):
            if slot in IN_PIECES:
                for source in range(4):
                    piece_copy(slot, source, way).wait_send()
            else:
                ring_copy(slot, way).wait_send()
            half_copy(slot, way).wait_send()
    total = packed[layer, core]
    for over, step, other in reversed(others):
        layer_copy(over, step, other).wait_recv()
        total += gathered[over * 4 + step, other]
    out_ref[0:16, :] = total[:, :WIDTH]
    out_ref[16:32, :] = total[:, WIDTH:]


def shards(train_grads, query_pre, basis_in, basis_out):
    dma = pltpu.SemaphoreType.DMA
    return pl.pallas_call(
        kernel,
        out_shape=jax.ShapeDtypeStruct((32, WIDTH), F32),
        in_specs=[
            pl.BlockSpec(memory_space=pl.ANY),
            pl.BlockSpec(memory_space=pl.ANY),
            pl.BlockSpec(memory_space=pl.ANY),
            pl.BlockSpec(memory_space=pl.ANY),
        ],
        out_specs=pl.BlockSpec(memory_space=pltpu.VMEM),
        scratch_shapes=[
            pltpu.VMEM((MODULES, WIDTH, WIDTH), BF16),
            pltpu.VMEM((MODULES, WIDTH, WIDTH), BF16),
            pltpu.VMEM((MODULES, OWN_TRAIN, FLAT), BF16),
            pltpu.VMEM((MODULES, OWN_TRAIN, FLAT), BF16),
            pltpu.VMEM((5, DEPTH, 64, FLAT), BF16),
            pltpu.VMEM((2, DEPTH, 64, REST), BF16),
            pltpu.VMEM((DEPTH, 64, SHARED), BF16),
            pltpu.VMEM((3, 256, FLAT), BF16),
            pltpu.VMEM((256, SHARED), BF16),
            pltpu.VMEM((2, 128, FLAT), BF16),
            pltpu.VMEM((2, 128, REST), BF16),
            pltpu.VMEM((256, 256), BF16),
            pltpu.VMEM((128, 64), BF16),
            pltpu.VMEM((64, 256), BF16),
            pltpu.VMEM((128, 256), F32),
            pltpu.VMEM((64, 64), BF16),
            pltpu.VMEM((64, 64), BF16),
            pltpu.VMEM((64, 64), BF16),
            pltpu.VMEM((2, 256, LANES), F32),
            pltpu.VMEM((256, LANES), F32),
            pltpu.VMEM((256, LANES), F32),
            pltpu.VMEM((LAYERS, 2, 16, LANES), F32),
            pltpu.VMEM((LAYERS, 2, 16, LANES), F32),
            dma((2,)), dma((MODULES,)), dma((SLOTS,)), dma((SLOTS,)),
            dma((SLOTS, 3)), dma((SLOTS, 3)), dma((2, 4, 2)), dma((2, 4, 2)), dma((SLOTS, 2)), dma((SLOTS, 2)), dma((SLOTS, 2)), dma((SLOTS, 2)),
            dma((SLOTS, 3)), dma((SLOTS, 3)), dma, dma, dma((LAYERS, 2)), dma((LAYERS, 2)), pltpu.SemaphoreType.REGULAR((3,)),
        ],
        compiler_params=pltpu.CompilerParams(
            collective_id=0, has_side_effects=True, vmem_limit_bytes=62 * 2**20
        ),
        name="influence_scores",
    )(jnp.transpose(train_grads, (1, 0, 2)), jnp.transpose(query_pre, (1, 0, 2)), basis_in, basis_out)


def solution(mesh):
    placed = (
        P("query", "layer", None),
        P("query", "layer", None),
        P("layer", None, None),
        P("layer", None, None),
    )
    return jax.shard_map(
        shards, mesh=mesh, in_specs=placed, out_specs=P("layer", "query"), check_vma=False
    )
```

```python
import jax
import jax.numpy as jnp
from jax import lax
from jax.experimental import pallas as pl
from jax.experimental.pallas import tpu as pltpu
from jax.sharding import PartitionSpec as P

MESH = pl.DeviceIdType.MESH
BF16 = jnp.bfloat16
F32 = jnp.float32

WIDTH = 64
FLAT = WIDTH * WIDTH
MODULES = 20
OWN_TRAIN = 16
LAYERS = 8
DEPTH = 4
SLOTS = 8
FIRST = 3
LAST = 6
EXTRA = 7
SHARED = 896
REST = FLAT - SHARED
IN_PIECES = (FIRST, 0)
FAR_FIRST = ((1, 2), (1, 1), (1, 3), (0, 2), (1, 0), (0, 1), (0, 3), (0, 0))
LANES = 128
PARTNERS = ((0, 1), (1, 0), (1, 1))


def dot(a, b):
    return jnp.dot(a, b, preferred_element_type=F32)


def dot_t(a, b):
    return lax.dot_general(a, b, (((1,), (1,)), ((), ())), preferred_element_type=F32)


def iota(shape, dim):
    return lax.broadcasted_iota(jnp.int32, shape, dim)


def one_hot(condition):
    return jnp.where(condition, 1.0, 0.0).astype(BF16)


def kernel(
    train_hbm, query_hbm, inner_hbm, outer_hbm, out_ref,
    inner_ref, outer_ref,
    train, rotated, full_blocks, rest_blocks, extra_blocks, pair_queries, extra_queries, column_queries, rest_queries,
    swap, spread_rows, spread_lanes, keep, columns_of, rows_even, rows_odd,
    pair_scores, column_scores, theirs, packed, gathered,
    basis_sem, train_sem, local_sem, local_query_sem,
    block_send, block_recv, piece_send, piece_recv, ring_send, ring_recv, half_send, half_recv,
    query_send, query_recv, pair_send, pair_recv, layer_send, layer_recv, told,
):
    layer = lax.axis_index("layer")
    place = lax.axis_index("query")
    z = place // 4
    column = (place // 2) % 2
    core = place % 2
    here = place % 4

    def at_plane(other_column, other_core):
        x = 1 - column if other_column else column
        c = 1 - core if other_core else core
        return x, c, (layer, z * 4 + x * 2 + c)

    def at_ring(step):
        return (layer, ((z + step + DEPTH) % DEPTH) * 4 + here)

    def layer_at(over, step):
        return (layer // 4 + over) % 2 * 4 + (layer + step) % 4

    def at_layer(over, step, other_core):
        c = 1 - core if other_core else core
        return (layer_at(over, step), z * 4 + column * 2 + c)

    near = (at_layer(0, 1, 0), at_layer(0, 3, 0), at_layer(1, 0, 0), at_layer(0, 0, 1))

    def tell(turn):
        for device in near:
            pl.semaphore_signal(told.at[turn], inc=1, device_id=device, device_id_type=MESH)

    def hear(turn):
        pl.semaphore_wait(told.at[turn], len(near))

    barrier = pltpu.get_barrier_semaphore()
    for partner in PARTNERS:
        pl.semaphore_signal(barrier, inc=1, device_id=at_plane(*partner)[2], device_id_type=MESH)
    for step in (1, -1):
        pl.semaphore_signal(barrier, inc=1, device_id=at_ring(step), device_id_type=MESH)
    for device in near[:3]:
        pl.semaphore_signal(barrier, inc=1, device_id=device, device_id_type=MESH)

    def load_train(m):
        return pltpu.make_async_copy(train_hbm.at[m], train.at[m], train_sem.at[m])

    def each_module(first, last, step):
        def body(m, carry):
            step(m)
            return carry

        lax.fori_loop(first, last, body, 0)

    base = 6 + 2 * FIRST
    load_inner = pltpu.make_async_copy(inner_hbm, inner_ref, basis_sem.at[0])
    load_outer = pltpu.make_async_copy(outer_hbm, outer_ref, basis_sem.at[1])
    load_train(base + core).start()
    load_inner.start()
    load_outer.start()
    load_train(base + 1 - core).start()
    each_module(0, base, lambda m: load_train(m).start())
    each_module(base + 2, MODULES, lambda m: load_train(m).start())

    row, col = iota((256, 256), 0), iota((256, 256), 1)
    swap[...] = one_hot((row // 16 == col % 16) & (row % 16 == col // 16))
    row, col = iota((128, 64), 0), iota((128, 64), 1)
    spread_rows[...] = one_hot(row % 64 == col)
    row, col = iota((64, 256), 0), iota((64, 256), 1)
    spread_lanes[...] = one_hot(col % 64 == row)
    row, col = iota((128, 256), 0), iota((128, 256), 1)
    group = col // 64
    keep[...] = jnp.where(((group == 0) | (group == 3)) == (row < 64), 1.0, 0.0)
    row, col = iota((64, 64), 0), iota((64, 64), 1)
    columns_of[...] = one_hot(col == 2 * (row % 32) + row // 32)
    rows_even[...] = one_hot(row == 2 * (col % 32) + col // 32)
    rows_odd[...] = one_hot(row == 2 * (col % 32) + 1 - col // 32)

    def side_by_side(pieces):
        return jnp.concatenate(pieces, axis=1)

    def stack(pieces):
        return jnp.concatenate(pieces, axis=0)

    def swap_rows(tile):
        pieces = side_by_side([stack([tile(16 * half + c) for c in range(16)]) for half in range(2)])
        return dot(swap[...], pieces).astype(BF16)

    def rotate(*modules):
        for m in modules:
            load_train(m).wait()
        values = [rotation(m) for m in modules]
        for m, value in zip(modules, values):
            rotated[m] = value

    def rotation(m):
        inner = dot(dot(spread_rows[...], inner_ref[m]).astype(BF16), spread_lanes[...])
        inner = (inner * keep[...]).astype(BF16)
        turned = dot_t(columns_of[...], outer_ref[m]).astype(BF16)
        outer = jnp.where(
            iota((64, 64), 0) < 32, dot(turned, rows_even[...]), dot(turned, rows_odd[...])
        ).astype(BF16)
        grads = train[m]
        rows = swap_rows(lambda c: grads[:, c * LANES:(c + 1) * LANES])
        matrices = stack(
            [rows[16 * e:16 * e + 16, h * LANES:(h + 1) * LANES] for e in range(OWN_TRAIN) for h in range(2)]
        )
        half = dot(matrices, inner).astype(BF16)
        stacked = stack(
            [
                side_by_side([half[32 * e:32 * e + 32, h * LANES:(h + 1) * LANES] for e in range(OWN_TRAIN)])
                for h in range(2)
            ]
        )
        both = dot(outer, stacked)
        first = iota((32, OWN_TRAIN * LANES), 1) % LANES < WIDTH
        result = jnp.where(first, both[:32], both[32:]).astype(BF16)
        pieces = side_by_side(
            [
                stack([result[16 * h:16 * h + 16, e * LANES:(e + 1) * LANES] for e in range(OWN_TRAIN)])
                for h in range(2)
            ]
        )
        final = dot(swap[...], pieces).astype(BF16)
        return side_by_side(
            [final[16 * c:16 * c + 16, h * LANES:(h + 1) * LANES] for h in range(2) for c in range(16)]
        )

    def is_pair(slot):
        return slot < 3 or slot == EXTRA

    def module_of(slot, x, c):
        if slot == EXTRA:
            return 16 + 2 * x + c
        return 4 * slot + 2 * x + c if is_pair(slot) else 6 + 2 * slot + c

    def entries(slot):
        if slot == EXTRA:
            return pl.ds(0, SHARED)
        return pl.ds(SHARED, REST) if slot >= 5 else pl.ds(0, FLAT)

    def blocks(slot):
        if slot == EXTRA:
            return extra_blocks
        return rest_blocks.at[slot - 5] if slot >= 5 else full_blocks.at[slot]

    def queries(slot):
        if is_pair(slot):
            return extra_queries if slot == EXTRA else pair_queries.at[slot]
        return rest_queries.at[slot - 5] if slot >= 5 else column_queries.at[slot - 3]

    def own_rows(count, first):
        return pl.ds(pl.multiple_of(first * count, count), count)

    def block_copy(slot, partner):
        x, c, device = at_plane(*PARTNERS[partner])
        return pltpu.make_async_remote_copy(
            src_ref=rotated.at[module_of(slot, x, c), :, entries(slot)],
            dst_ref=blocks(slot).at[z, own_rows(16, here)],
            send_sem=block_send.at[slot, partner],
            recv_sem=block_recv.at[slot, partner],
            device_id=device,
            device_id_type=MESH,
        )

    def own_copy(slot):
        return pltpu.make_async_copy(
            rotated.at[module_of(slot, column, core), :, entries(slot)],
            blocks(slot).at[z, own_rows(16, here)],
            local_sem.at[slot],
        )

    def ring_copy(slot, way):
        return pltpu.make_async_remote_copy(
            src_ref=blocks(slot).at[z],
            dst_ref=blocks(slot).at[z],
            send_sem=ring_send.at[slot, way],
            recv_sem=ring_recv.at[slot, way],
            device_id=at_ring(1 - 2 * way),
            device_id_type=MESH,
        )

    def half_copy(slot, way):
        source = (z + DEPTH - 1 + 2 * way) % DEPTH
        half = blocks(slot).at[source, pl.ds(32 * way, 32)]
        return pltpu.make_async_remote_copy(
            src_ref=half,
            dst_ref=half,
            send_sem=half_send.at[slot, way],
            recv_sem=half_recv.at[slot, way],
            device_id=at_ring(1 - 2 * way),
            device_id_type=MESH,
        )

    def query_copy(slot, partner):
        x, c, device = at_plane(*PARTNERS[partner])
        return pltpu.make_async_remote_copy(
            src_ref=query_hbm.at[module_of(slot, x, c), :, entries(slot)],
            dst_ref=queries(slot).at[own_rows(64, PARTNERS[partner][0] * 2 + core)],
            send_sem=query_send.at[slot, partner],
            recv_sem=query_recv.at[slot, partner],
            device_id=device,
            device_id_type=MESH,
        )

    def own_query_copy(slot):
        return pltpu.make_async_copy(
            query_hbm.at[module_of(slot, column, core), :, entries(slot)],
            queries(slot).at[own_rows(64, core)],
            local_query_sem.at[slot],
        )

    def piece_copy(slot, source, way, held=None):
        target = blocks(slot).at[z, own_rows(16, source)]
        return pltpu.make_async_remote_copy(
            src_ref=target if held is None else held,
            dst_ref=target,
            send_sem=piece_send.at[IN_PIECES.index(slot), source, way],
            recv_sem=piece_recv.at[IN_PIECES.index(slot), source, way],
            device_id=at_ring(1 - 2 * way),
            device_id_type=MESH,
        )

    def query_partners(slot):
        return (1, 2, 0) if is_pair(slot) else (0,)

    def send_queries(slot):
        for partner in query_partners(slot):
            query_copy(slot, partner).start()
        own_query_copy(slot).start()

    def send_blocks(slot):
        for partner in (1, 2, 0):
            block_copy(slot, partner).start()
        if slot in IN_PIECES:
            for way in range(2):
                piece_copy(slot, here, way, rotated.at[module_of(slot, column, core)]).start()
        own_copy(slot).start()

    def send_piece(slot, partner):
        block_copy(slot, partner).wait_recv()
        x, c, _ = at_plane(*PARTNERS[partner])
        for way in range(2):
            piece_copy(slot, 2 * x + c, way).start()

    def send_ring(slot):
        for partner in range(3):
            block_copy(slot, partner).wait_recv()
        own_copy(slot).wait()
        for way in range(2):
            ring_copy(slot, way).start()

    def send_half(slot):
        for way in range(2):
            if slot in IN_PIECES:
                for source in range(4):
                    piece_copy(slot, source, way).wait_recv()
            else:
                ring_copy(slot, way).wait_recv()
            half_copy(slot, way).start()

    load_inner.wait()
    load_outer.wait()
    rotate(base, base + 1)
    pl.semaphore_wait(barrier, len(PARTNERS) + 2 + 3)
    send_blocks(3)
    tell(0)
    rotate(0, 1)
    send_piece(3, 0)
    rotate(2, 3)
    send_blocks(0)
    send_piece(3, 1)
    rotate(4, 5)
    send_piece(3, 2)
    send_piece(0, 0)
    rotate(6, 7)
    send_blocks(1)
    send_piece(0, 1)
    rotate(8, 9)
    send_piece(0, 2)
    rotate(10, 11)
    send_blocks(2)
    hear(0)
    tell(1)
    for slot in (3, 4, 5, 6):
        send_queries(slot)
    send_half(3)
    rotate(16, 17)
    rotate(18, 19)
    send_blocks(7)
    rotate(14, 15)
    send_blocks(4)
    send_blocks(5)
    send_blocks(6)
    send_queries(0)
    send_ring(1)
    hear(1)
    tell(2)

    def wait_blocks(slot):
        for way in range(2):
            half_copy(slot, way).wait_recv()
        if slot in IN_PIECES:
            own_copy(slot).wait()
        wait_queries(slot)

    def wait_queries(slot):
        for partner in query_partners(slot):
            query_copy(slot, partner).wait_recv()
        own_query_copy(slot).wait()

    pair_scores[...] = jnp.zeros_like(pair_scores)
    column_scores[...] = jnp.zeros_like(column_scores)

    def score(slot):
        wait_blocks(slot)
        rows = blocks(slot)[...]
        scores = dot_t(rows.reshape(256, rows.shape[2]), queries(slot)[...])
        if is_pair(slot):
            for side in range(2):
                pair_scores[side] += scores[:, side * LANES:(side + 1) * LANES]
        else:
            column_scores[...] += scores

    def score_part(step):
        source = (z + step) % DEPTH
        rows = pl.ds(pl.multiple_of(source * 64, 64), 64)
        column_scores[rows, :] += dot_t(blocks(LAST)[source], queries(LAST)[...])

    send_ring(2)
    send_half(0)
    send_ring(7)
    send_half(1)
    send_ring(4)
    send_queries(1)
    send_queries(7)
    score(3)
    hear(2)
    send_half(2)
    send_ring(5)
    send_queries(2)
    send_half(7)
    send_ring(6)
    send_half(4)
    score(0)
    score(1)
    send_half(5)
    score(4)
    score(7)
    send_half(6)
    score(2)

    cross = pltpu.make_async_remote_copy(
        src_ref=pair_scores.at[1],
        dst_ref=theirs,
        send_sem=pair_send,
        recv_sem=pair_recv,
        device_id=at_plane(1, 0)[2],
        device_id_type=MESH,
    )
    cross.start()
    score(5)
    wait_queries(LAST)
    for step in (0, 1, 3):
        score_part(step)
    def layer_copy(over, step, other):
        return pltpu.make_async_remote_copy(
            src_ref=packed.at[layer_at(over, step), 1 - core if other else core],
            dst_ref=gathered.at[over * 4 + step, other],
            send_sem=layer_send.at[over * 4 + step, other],
            recv_sem=layer_recv.at[over * 4 + step, other],
            device_id=at_layer(over, step, other),
            device_id_type=MESH,
        )

    def pack(first, count):
        rows = pl.ds(pl.multiple_of(first * 32, 32), count * 32)
        own = pair_scores[0, rows, :] + column_scores[rows, :] + theirs[rows, :]
        moved = pltpu.roll(own, WIDTH, 1)
        left = iota((count, 16, LANES), 2) < WIDTH
        own = own.reshape(count, 2, 16, LANES)
        moved = moved.reshape(count, 2, 16, LANES)
        packed[pl.ds(first, count), 0] = jnp.where(left, own[:, 0], moved[:, 1])
        packed[pl.ds(first, count), 1] = jnp.where(left, moved[:, 0], own[:, 1])

    others = [(over, step, other) for over, step in FAR_FIRST for other in (1, 0) if over or step or other]
    opposite = (z + 2) % DEPTH

    def start_sums(late):
        for over, step in FAR_FIRST:

            @pl.when((layer_at(over, step) // 2 == opposite) == late)
            def _():
                for other in (1, 0):
                    if over or step or other:
                        layer_copy(over, step, other).start()

    cross.wait_recv()
    pack(0, LAYERS)
    start_sums(False)
    for way in range(2):
        half_copy(LAST, way).wait_recv()
    score_part(2)
    pack(2 * opposite, 2)
    start_sums(True)
    for each in others:
        layer_copy(*each).wait_send()
    cross.wait_send()
    for slot in range(SLOTS):
        for partner in range(3):
            block_copy(slot, partner).wait_send()
        for partner in query_partners(slot):
            query_copy(slot, partner).wait_send()
        for way in range(2):
            if slot in IN_PIECES:
                for source in range(4):
                    piece_copy(slot, source, way).wait_send()
            else:
                ring_copy(slot, way).wait_send()
            half_copy(slot, way).wait_send()
    total = packed[layer, core]
    for over, step, other in reversed(others):
        layer_copy(over, step, other).wait_recv()
        total += gathered[over * 4 + step, other]
    out_ref[0:16, :] = total[:, :WIDTH]
    out_ref[16:32, :] = total[:, WIDTH:]


def shards(train_grads, query_pre, basis_in, basis_out):
    dma = pltpu.SemaphoreType.DMA
    return pl.pallas_call(
        kernel,
        out_shape=jax.ShapeDtypeStruct((32, WIDTH), F32),
        in_specs=[
            pl.BlockSpec(memory_space=pl.ANY),
            pl.BlockSpec(memory_space=pl.ANY),
            pl.BlockSpec(memory_space=pl.ANY),
            pl.BlockSpec(memory_space=pl.ANY),
        ],
        out_specs=pl.BlockSpec(memory_space=pltpu.VMEM),
        scratch_shapes=[
            pltpu.VMEM((MODULES, WIDTH, WIDTH), BF16),
            pltpu.VMEM((MODULES, WIDTH, WIDTH), BF16),
            pltpu.VMEM((MODULES, OWN_TRAIN, FLAT), BF16),
            pltpu.VMEM((MODULES, OWN_TRAIN, FLAT), BF16),
            pltpu.VMEM((5, DEPTH, 64, FLAT), BF16),
            pltpu.VMEM((2, DEPTH, 64, REST), BF16),
            pltpu.VMEM((DEPTH, 64, SHARED), BF16),
            pltpu.VMEM((3, 256, FLAT), BF16),
            pltpu.VMEM((256, SHARED), BF16),
            pltpu.VMEM((2, 128, FLAT), BF16),
            pltpu.VMEM((2, 128, REST), BF16),
            pltpu.VMEM((256, 256), BF16),
            pltpu.VMEM((128, 64), BF16),
            pltpu.VMEM((64, 256), BF16),
            pltpu.VMEM((128, 256), F32),
            pltpu.VMEM((64, 64), BF16),
            pltpu.VMEM((64, 64), BF16),
            pltpu.VMEM((64, 64), BF16),
            pltpu.VMEM((2, 256, LANES), F32),
            pltpu.VMEM((256, LANES), F32),
            pltpu.VMEM((256, LANES), F32),
            pltpu.VMEM((LAYERS, 2, 16, LANES), F32),
            pltpu.VMEM((LAYERS, 2, 16, LANES), F32),
            dma((2,)), dma((MODULES,)), dma((SLOTS,)), dma((SLOTS,)),
            dma((SLOTS, 3)), dma((SLOTS, 3)), dma((2, 4, 2)), dma((2, 4, 2)), dma((SLOTS, 2)), dma((SLOTS, 2)), dma((SLOTS, 2)), dma((SLOTS, 2)),
            dma((SLOTS, 3)), dma((SLOTS, 3)), dma, dma, dma((LAYERS, 2)), dma((LAYERS, 2)), pltpu.SemaphoreType.REGULAR((3,)),
        ],
        compiler_params=pltpu.CompilerParams(
            collective_id=0, has_side_effects=True, vmem_limit_bytes=62 * 2**20
        ),
        name="influence_scores",
    )(jnp.transpose(train_grads, (1, 0, 2)), jnp.transpose(query_pre, (1, 0, 2)), basis_in, basis_out)


def solution(mesh):
    placed = (
        P("query", "layer", None),
        P("query", "layer", None),
        P("layer", None, None),
        P("layer", None, None),
    )
    return jax.shard_map(
        shards, mesh=mesh, in_specs=placed, out_specs=P("layer", "query"), check_vma=False
    )
```
